256 devices in a mesh: section: 8 (over x_lo, y), tensor: 32 (over z, x_hi, core).
Axes of the slice: x: 4 (x_hi: 2, x_lo: 2; x = x_hi * 2 + x_lo), y: 4, z: 8, core: 2. Of those that a mesh axis runs over, the one named last changes fastest.
Arguments:
- fwd_in: bfloat16 [8, 256, 8192], P('section', 'tensor'), may hold values from -6 to 6
- saved_in: bfloat16 [8, 256, 8192], P('section', 'tensor'), may hold values from -6 to 6
- grad_in: bfloat16 [8, 256, 8192], P('section', 'tensor'), may hold values from -6 to 6
- norm_gain: float32 [8, 8192], P('section'), may hold values from 0.5 to 1.5
- query_weight: bfloat16 [8, 8192, 8192], P('section', None, 'tensor'), may hold values from -2 to 2
- keyval_weight: bfloat16 [8, 8192, 2048], P('section', None, 'tensor'), may hold values from -1 to 1
- out_weight: bfloat16 [8, 8192, 8192], P('section', 'tensor'), may hold values from -0.0625 to 0.0625
- encoder: float32 [64, 128, 32], replicated, may hold values from -0.5 to 0.5
- decoder: float32 [64, 32, 128], replicated, may hold values from -1 to 1
- seq_pos: int32 [256], replicated, may hold values from 0 to 255, each once
- rope_ids: int32 [256], replicated, may hold values from 0 to 4095
Outputs:
- section_out: bfloat16 [8, 256, 8192], P('section', 'tensor')
- act_sent: bfloat16 [8, 256, 8192], P('section', 'tensor')
- input_grad: bfloat16 [8, 256, 8192], P('section', 'tensor')
- grad_sent: bfloat16 [8, 256, 8192], P('section', 'tensor')
The draws below stay inside these ranges and needn't reach their ends.
Inputs may be any that keep to these rules, and one draw needn't show every extreme that they name: `seq_pos`: a permutation of the 256 positions.
All inputs are finite; a program needn't handle non-finite values.
Results may differ from the reference program's by a relative error of at most 0.022.
Values may be sent and summed in bfloat16 or wider, within the bound.
A program may use at most 128 MiB of HBM per device.

```python
import math
import jax
import jax.numpy as jnp
from jax import lax

D = 8192
HD = 128
KVH = 8
QH = 64
ENC = 2048
ENC_BLOCKS = 64
CONTEXT = 4096
TOKENS = 256
SECTIONS = 8


def common_keys(key):
    return jnp.clip(jax.random.normal(key, (SECTIONS, D, 2 * KVH * HD), jnp.float32), -6.0, 6.0)


def draw_keyval_weight(key, part):
    base = common_keys(key)
    return (base * D ** (-0.5)).astype(jnp.bfloat16)


def draw_query_weight(key, part):
    key = jax.random.fold_in(key, 23)
    shape = (SECTIONS, D, QH * HD)
    fresh = jnp.clip(jax.random.normal(key, shape, jnp.float32), -6.0, 6.0) * D ** (-0.5)
    return fresh.astype(jnp.bfloat16)


def with_ends(drawn, stream_key, smallest, largest):
    extent = drawn.shape
    index_at = [jax.random.randint(jax.random.fold_in(stream_key, axis), (), 0, extent[axis]) for axis in range(len(extent))]
    drawn = drawn.at[tuple(index_at)].set(smallest)
    longest = extent.index(max(extent))
    index_at[longest] = (index_at[longest] + 1) % extent[longest]
    return drawn.at[tuple(index_at)].set(largest)


def level_of(rng, extent, shards, low, high):
    gain, own = 1.0, jax.random.fold_in(rng, 6)
    for axis_at, blocks in shards:
        heights = jnp.exp(jax.random.uniform(jax.random.fold_in(own, axis_at), (blocks,), jnp.float32, low / len(shards), high / len(shards)))
        gain = gain * jnp.repeat(heights, extent[axis_at] // blocks).reshape([-1 if axis == axis_at else 1 for axis in range(len(extent))])
    return gain


def noise(rng, extent, deviation, limit, cuts=(), kind=jnp.bfloat16):
    factor_of = level_of(rng, extent, cuts, -0.22, 0.18) if cuts else 1.0
    array = jax.random.normal(rng, extent, jnp.float32) * deviation * factor_of
    return jnp.minimum(jnp.maximum(array, -limit), limit).astype(kind)


def setup_inputs(seed: int = 0) -> dict:
    streams_of = jax.random.split(jax.random.key(seed), 12)
    fwd_in = noise(streams_of[0], (SECTIONS, TOKENS, D), 1.0, 6.0, ((0, 8), (1, 32)))
    saved_in = noise(streams_of[1], (SECTIONS, TOKENS, D), 1.0, 6.0, ((0, 8), (1, 32)))
    grad_in = noise(streams_of[2], (SECTIONS, TOKENS, D), 1.0, 6.0, ((0, 8), (1, 32)))
    norm_gain = jnp.clip(1.0 + 0.1 * jax.random.normal(streams_of[3], (SECTIONS, D), jnp.float32), 0.5, 1.5)
    query_weight = draw_query_weight(jax.random.fold_in(streams_of[11], 71), 0)
    keyval_weight = draw_keyval_weight(jax.random.fold_in(streams_of[11], 71), 0)
    out_weight = noise(streams_of[6], (SECTIONS, QH * HD, D), (QH * HD) ** -0.5, 0.0625, ((0, 8), (1, 32)))
    encoder = noise(streams_of[7], (ENC_BLOCKS, D // ENC_BLOCKS, ENC // ENC_BLOCKS), (D // ENC_BLOCKS) ** -0.5, 0.5, (), jnp.float32)
    decoder = noise(streams_of[8], (ENC_BLOCKS, ENC // ENC_BLOCKS, D // ENC_BLOCKS), (ENC // ENC_BLOCKS) ** -0.5, 1.0, (), jnp.float32)
    seq_pos = jax.random.permutation(streams_of[9], TOKENS).astype(jnp.int32)
    rope_ids = with_ends(jax.random.randint(streams_of[10], (TOKENS,), 0, CONTEXT), jax.random.fold_in(streams_of[10], 1), 0, CONTEXT - 1).astype(jnp.int32)
    return dict(fwd_in=fwd_in, saved_in=saved_in, grad_in=grad_in, norm_gain=norm_gain, query_weight=query_weight, keyval_weight=keyval_weight, out_weight=out_weight, encoder=encoder, decoder=decoder, seq_pos=seq_pos, rope_ids=rope_ids)


EPSILON = 1e-05
ROPE_BASE = 10000.0
NEG_FILL = -1e+30

def angle_tables(position_ids, head_size):
    pair_index = jnp.arange(head_size // 2, dtype=jnp.float32)
    frequency = ROPE_BASE ** (-2.0 * pair_index / head_size)
    angle_grid = position_ids.astype(jnp.float32)[:, None] * frequency[None, :]
    return (jnp.cos(angle_grid), jnp.sin(angle_grid))

def rotate_heads(values, cosine, sine_part):
    shaped = values.reshape(values.shape[0], values.shape[1], -1, 2)
    even_part = shaped[..., 0]
    odd_part = shaped[..., 1]
    cos_grid = cosine[:, None, :]
    sin_grid = sine_part[:, None, :]
    turned = jnp.stack([even_part * cos_grid - odd_part * sin_grid, odd_part * cos_grid + even_part * sin_grid], axis=-1)
    return turned.reshape(values.shape)

def encode_blocks(values, encoder):
    grouped = values.reshape(values.shape[0], encoder.shape[0], -1)
    mapped = jnp.einsum('tbi,bio->tbo', grouped, encoder, precision=lax.Precision.HIGHEST)
    return mapped.reshape(values.shape[0], -1)

def decode_blocks(values, decoder):
    grouped = values.reshape(values.shape[0], decoder.shape[0], -1)
    mapped = jnp.einsum('tbi,bio->tbo', grouped, decoder, precision=lax.Precision.HIGHEST)
    return mapped.reshape(values.shape[0], -1)

def normalize(activation, gain_row):
    floated = activation.astype(jnp.float32)
    factor = lax.rsqrt(lax.optimization_barrier(jnp.mean(floated * floated, axis=-1, keepdims=True)) + EPSILON)
    return (floated, factor, (floated * factor * gain_row).astype(jnp.bfloat16))

def attend_parts(activation, gain_row, query_matrix, keyval_matrix, seq_pos, rope_ids):
    floated, factor, normed = normalize(activation, gain_row)
    cosine, sine_part = angle_tables(rope_ids, HD)
    tokens = activation.shape[0]
    query_raw = jnp.dot(normed, query_matrix, preferred_element_type=jnp.float32).reshape(tokens, QH, HD)
    query = rotate_heads(query_raw, cosine, sine_part).astype(jnp.bfloat16)
    keyval_raw = jnp.dot(normed, keyval_matrix, preferred_element_type=jnp.float32).reshape(tokens, KVH, 2, HD)
    key_rows = rotate_heads(keyval_raw[:, :, 0], cosine, sine_part).astype(jnp.bfloat16)
    value_rows = keyval_raw[:, :, 1].astype(jnp.bfloat16)
    group_size = QH // KVH
    key_rep = jnp.repeat(key_rows, group_size, axis=1)
    value_rep = jnp.repeat(value_rows, group_size, axis=1)
    scores = jnp.einsum('thd,shd->hts', query.astype(jnp.float32), key_rep.astype(jnp.float32)) / math.sqrt(HD)
    visible = seq_pos[None, :] <= seq_pos[:, None]
    masked = jnp.where(visible[None], scores, NEG_FILL)
    highest = lax.optimization_barrier(jnp.max(masked, axis=-1, keepdims=True))
    raised = jnp.exp(masked - highest)
    weighting = raised / lax.optimization_barrier(jnp.sum(raised, axis=-1, keepdims=True))
    rounded_weighting = weighting.astype(jnp.bfloat16)
    attended = jnp.einsum('hts,shd->thd', rounded_weighting.astype(jnp.float32), value_rep.astype(jnp.float32))
    attended = attended.astype(jnp.bfloat16).reshape(tokens, QH * HD)
    return (floated, factor, cosine, sine_part, query, key_rep, value_rep, weighting, rounded_weighting, attended)

def reference(fwd_in, saved_in, grad_in, norm_gain, query_weight, keyval_weight, out_weight, encoder, decoder, seq_pos, rope_ids):
    section_list = []
    packed_list = []
    input_list = []
    backpack_list = []
    group_size = QH // KVH
    for section_index in range(SECTIONS):
        gain_row = norm_gain[section_index]
        parts = attend_parts(fwd_in[section_index], gain_row, query_weight[section_index], keyval_weight[section_index], seq_pos, rope_ids)
        floated = parts[0]
        attended = parts[-1]
        projected = jnp.dot(attended, out_weight[section_index], preferred_element_type=jnp.float32)
        section_out = (floated + decode_blocks(encode_blocks(projected, encoder), decoder)).astype(jnp.bfloat16)
        section_list.append(section_out)
        packed_list.append(encode_blocks(section_out.astype(jnp.float32), encoder).astype(jnp.bfloat16))
        floated, factor, cosine, sine_part, query, key_rep, value_rep, weighting, rounded_weighting, attended = attend_parts(saved_in[section_index], gain_row, query_weight[section_index], keyval_weight[section_index], seq_pos, rope_ids)
        tokens = floated.shape[0]
        gradient = grad_in[section_index]
        grad_att = jnp.dot(gradient, out_weight[section_index].T, preferred_element_type=jnp.float32)
        grad_att = grad_att.astype(jnp.bfloat16).reshape(tokens, QH, HD)
        prob_grad = jnp.einsum('thd,shd->hts', grad_att.astype(jnp.float32), value_rep.astype(jnp.float32))
        score_grad = weighting * (prob_grad - lax.optimization_barrier(jnp.sum(weighting * prob_grad, axis=-1, keepdims=True))) / math.sqrt(HD)
        score_grad = score_grad.astype(jnp.bfloat16)
        query_grad = jnp.einsum('hts,shd->thd', score_grad.astype(jnp.float32), key_rep.astype(jnp.float32))
        query_grad = rotate_heads(query_grad, cosine, -sine_part).astype(jnp.bfloat16)
        key_each = jnp.einsum('hts,thd->shd', score_grad.astype(jnp.float32), query.astype(jnp.float32))
        value_each = jnp.einsum('hts,thd->shd', rounded_weighting.astype(jnp.float32), grad_att.astype(jnp.float32))
        key_sum = rotate_heads(lax.optimization_barrier(jnp.sum(key_each.reshape(tokens, KVH, group_size, HD), axis=2)), cosine, -sine_part)
        value_sum = lax.optimization_barrier(jnp.sum(value_each.reshape(tokens, KVH, group_size, HD), axis=2))
        keyval_grad = jnp.stack([key_sum, value_sum], axis=2).reshape(tokens, 2 * KVH * HD).astype(jnp.bfloat16)
        normed_grad = jnp.dot(query_grad.reshape(tokens, QH * HD), query_weight[section_index].T, preferred_element_type=jnp.float32)
        normed_grad = normed_grad + jnp.dot(keyval_grad, keyval_weight[section_index].T, preferred_element_type=jnp.float32)
        recovered = decode_blocks(encode_blocks(normed_grad, encoder), decoder)
        scaled = recovered * gain_row
        correction = factor * (scaled - floated * factor * factor * lax.optimization_barrier(jnp.mean(scaled * floated, axis=-1, keepdims=True)))
        input_grad = (gradient.astype(jnp.float32) + correction).astype(jnp.bfloat16)
        input_list.append(input_grad)
        backpack_list.append(encode_blocks(input_grad.astype(jnp.float32), encoder).astype(jnp.bfloat16))
    zeros_like = jnp.zeros_like(fwd_in[0])
    act_list = [zeros_like]
    for section_index in range(1, SECTIONS):
        act_list.append(decode_blocks(packed_list[section_index - 1].astype(jnp.float32), decoder).astype(jnp.bfloat16))
    back_list = []
    for section_index in range(SECTIONS - 1):
        back_list.append(decode_blocks(backpack_list[section_index + 1].astype(jnp.float32), decoder).astype(jnp.bfloat16))
    back_list.append(zeros_like)
    return (jnp.stack(section_list), jnp.stack(act_list), jnp.stack(input_list), jnp.stack(back_list))
```

```python
import math

import jax
import jax.numpy as jnp
from jax import lax
from jax.experimental import pallas as pl
from jax.experimental.pallas import tpu as pltpu
from jax.sharding import PartitionSpec as P

MESH = pl.DeviceIdType.MESH
HD = 128
D = 8192
HALF = D // 2
ENC = 2048
T = 256
EPSILON = 1e-05
ROPE_BASE = 10000.0
NEG_FILL = -1e30
SCALE = 1.0 / math.sqrt(HD)
F32 = jnp.float32
BF16 = jnp.bfloat16
SAVED, GRAD, FWD = 0, 1, 2

KEYS = [(0, 1), (0, -1), (0, 2), (0, -2), (0, 3), (0, -3), (0, 4, 0), (0, 4, 1)]
KEYS += [(1, 0), (1, 1), (1, -1), (1, 2), (1, -2), (1, 3), (1, -3), (1, 4, 0), (1, 4, 1)]
BLOCKS = [(0, 0)] + [k for k in KEYS if len(k) == 2] + [(0, 4), (1, 4)]
GROUPS = [
    ([], [("M", (0, 0), (0, 1)), ("P", (0, 0), (0, -1)), ("X", (0, 0), (1, 0))], [(0, 0)]),
    (
        [(0, 1), (0, -1)],
        [("M", (0, 1), (0, 2)), ("P", (0, -1), (0, -2)), ("X", (0, 1), (1, 1)), ("X", (0, -1), (1, -1))],
        [(0, 1), (0, -1)],
    ),
    ([(1, 0)], [], [(1, 0)]),
    (
        [(0, 2), (0, -2)],
        [("M", (0, 2), (0, 3)), ("P", (0, -2), (0, -3)), ("X", (0, 2), (1, 2)), ("X", (0, -2), (1, -2))],
        [(0, 2), (0, -2)],
    ),
    ([(1, 1), (1, -1)], [], [(1, 1), (1, -1)]),
    ([(0, 3), (0, -3)], [("M", (0, 3), (0, 4, 0)), ("P", (0, -3), (0, 4, 1))], [(0, 3), (0, -3)]),
    ([(1, 2)], [("M", (1, 2), (1, 3))], [(1, 2)]),
    ([(1, -2)], [("P", (1, -2), (1, -3))], [(1, -2)]),
    ([(0, 4, 0), (0, 4, 1)], [], [(0, 4)]),
    ([(1, 3), (1, -3)], [("M", (1, 3), (1, 4, 0)), ("P", (1, -3), (1, 4, 1))], [(1, 3), (1, -3)]),
    ([(1, 4, 0), (1, 4, 1)], [], [(1, 4)]),
]
OFFSETS = (0.0, 4.1, 8.2)
TASKS = [(1.5, "enc"), (4.05, "woe"), (7.05, "qe"), (10.05, "projS"), (12.5, "attS"), (14.15, "gatt"), (14.3, "bwd")]
TASKS += [(15.3, "kvsum"), (15.4, "rsb0"), (16.3, "rsb1"), (19.0, "fwd")]
ORDER = [(i + off, a) for a, off in enumerate(OFFSETS) for i in range(len(GROUPS))] + TASKS
ORDER = [item for _, item in sorted(ORDER, key=lambda entry: entry[0])]


def mm(a, b):
    return jnp.dot(a, b, preferred_element_type=F32)


def mm_nt(a, b):
    return lax.dot_general(a, b, (((1,), (1,)), ((), ())), preferred_element_type=F32)


def rotate(x, cosine, sine):
    lane = lax.broadcasted_iota(jnp.int32, x.shape, 1)
    swapped = jnp.where(lane % 2 == 0, pltpu.roll(x, x.shape[1] - 1, 1), pltpu.roll(x, 1, 1))
    return x * cosine + swapped * sine


def kernel(
    fwd_ref, saved_ref, grad_ref, gain_ref, cos_ref, sin_ref, kvcos_ref, kvsin_ref, seqc_ref, seqr_ref,
    wq_hbm, wkv_hbm, wo_hbm, enc_hbm, dec_hbm,
    out_ref, act_ref, ig_ref, gs_ref,
    G, wq, wkv, wo, enc_raw, dec_raw, enc_bd, enc_t, dec_bd, woe, qe, kve,
    nrm, chipf, factor_ref, accq, acckv, accg, kvt, qrot, qtr, gab, gatr, prob, att, qg, kvg, kgs, kgr,
    rsb, r1, r2, r3, pk_s, pk_r, scaled_ref,
    wsem, st_s, st_r, g_s, g_r, sb_s, sb_r, kv_s, kv_r, kg_s, kg_r, rs_s, rs_r, sc_s, sc_r,
):
    s = lax.axis_index("section")
    t = lax.axis_index("tensor")
    z, h, c = t // 4, (t // 2) % 2, t % 2
    j = t % 4

    def tid(zz, hh, cc):
        return (s, zz * 4 + hh * 2 + cc)

    def zmod(d):
        return lax.rem(z + d + 8, 8)

    sib = tid(z, h, 1 - c)
    link = {"M": tid(zmod(-1), h, c), "P": tid(zmod(1), h, c), "X": tid(z, 1 - h, c)}
    group = [sib, link["X"], tid(z, 1 - h, 1 - c)]
    nxt, prv = (lax.rem(s + 1, 8), t), (lax.rem(s + 7, 8), t)
    along = [tid(zmod(k), h, c) for k in range(1, 8)]

    loads = []
    for i, (src, dst) in enumerate([(enc_hbm, enc_raw), (dec_hbm, dec_raw), (wo_hbm, wo), (wq_hbm, wq), (wkv_hbm, wkv)]):
        loads.append(pltpu.make_async_copy(src, dst, wsem.at[i]))
        loads[-1].start()

    barrier = pltpu.get_barrier_semaphore()
    for peer in along + group + [nxt, prv]:
        pl.semaphore_signal(barrier, inc=1, device_id=peer, device_id_type=MESH)

    def put_own(a, values):
        nrm[a, 0] = values[:, :HALF]
        nrm[a, 1] = values[:, HALF:]

    def normed(ref, slot):
        x = ref[...].astype(F32)
        factor = lax.rsqrt(jnp.mean(x * x, axis=-1, keepdims=True) + EPSILON)
        if slot is not None:
            factor_ref[...] = jnp.broadcast_to(factor, factor_ref.shape)
        return x * factor * gain_ref[...]

    pending = []

    def send(src, dst, ssem, rsem, peer):
        copy = pltpu.make_async_remote_copy(
            src_ref=src, dst_ref=dst, send_sem=ssem, recv_sem=rsem, device_id=peer, device_id_type=MESH
        )
        copy.start()
        pending.append(copy)

    def arrived(dst, ssem, rsem, peer):
        pltpu.make_async_remote_copy(
            src_ref=dst, dst_ref=dst, send_sem=ssem, recv_sem=rsem, device_id=peer, device_id_type=MESH
        ).wait_recv()

    put_own(SAVED, normed(saved_ref, 0))
    pl.semaphore_wait(barrier, len(along) + len(group) + 2)

    def stage(a):
        send(nrm.at[a, 1 - c], chipf.at[a, c], st_s.at[a], st_r.at[a], sib)

    stage(SAVED)
    put_own(GRAD, grad_ref[...].astype(F32))
    stage(GRAD)
    put_own(FWD, normed(fwd_ref, None))
    stage(FWD)

    def where(key):
        column = h if key[0] == 0 else 1 - h
        return column * 8 + zmod(key[1])

    def piece(a, half, key):
        ref = G.at[a, half, where(key)]
        if len(key) == 3:
            ref = ref.at[:, pl.ds(key[2] * (HALF // 2), HALF // 2)]
        return ref

    def form_own(a):
        arrived(chipf.at[a, 1 - c], st_s.at[a], st_r.at[a], sib)
        chipf[a, c] = nrm[a, c]
        G[a, c, h * 8 + z] = chipf[a].reshape(16, HALF).astype(BF16)

    def step(a, g):
        waits, sends, ready = GROUPS[g]
        if g == 0:
            form_own(a)
        for key in waits:
            i = KEYS.index(key)
            arrived(piece(a, c, key), g_s.at[a, i], g_r.at[a, i], link["M"])
        for way, here, there in sends:
            i = KEYS.index(there)
            part = piece(a, c, here + there[2:])
            send(part, part, g_s.at[a, i], g_r.at[a, i], link[way])
        for key in ready:
            i = BLOCKS.index(key)
            send(piece(a, c, key), piece(a, c, key), sb_s.at[a, i], sb_r.at[a, i], sib)

    def whole(a):
        for i, key in enumerate(BLOCKS):
            arrived(piece(a, 1 - c, key), sb_s.at[a, i], sb_r.at[a, i], sib)

    def make_enc():
        loads[0].wait()
        loads[1].wait()

        def fill(i, _):
            e = enc_raw[pl.ds(i * 512, 512), :]
            wide = jnp.concatenate([e, e, e, e], axis=1)
            row = lax.broadcasted_iota(jnp.int32, (512, 128), 0) // 128
            col = lax.broadcasted_iota(jnp.int32, (512, 128), 1) // 32
            wide = jnp.where(row == col, wide, 0.0)
            enc_bd[pl.ds(i * 512, 512), :] = wide.astype(BF16)
            enc_t[pl.ds(i * 128, 128), :] = wide.T.astype(BF16)
            d = dec_raw[pl.ds(i * 128, 128), :]
            drow = lax.broadcasted_iota(jnp.int32, (128, 128), 0) // 32
            parts = [jnp.where(drow == q, d, 0.0) for q in range(4)]
            dec_bd[pl.ds(i * 128, 128), :] = jnp.concatenate(parts, axis=1).astype(BF16)
            return 0

        lax.fori_loop(0, 16, fill, 0)

    def make_woe():
        loads[2].wait()

        def fill(i, _):
            cols = pl.ds(pl.multiple_of(i * 512, 512), 512)
            outs = pl.ds(pl.multiple_of(i * 128, 128), 128)
            woe[:, outs] = mm(wo[:, cols], enc_bd[pl.ds(i * 512, 512), :]).astype(BF16)
            return 0

        lax.fori_loop(0, 16, fill, 0)

    def make_qe():
        loads[3].wait()
        loads[4].wait()

        def fill(i, _):
            rows, outs = pl.ds(i * 512, 512), pl.ds(i * 128, 128)
            e = enc_t[outs, :]
            qe[outs, :] = mm(e, wq[rows, :]).astype(BF16)
            kve[outs, :] = mm(e, wkv[rows, :]).astype(BF16)
            return 0

        lax.fori_loop(0, 16, fill, 0)

    def each_chunk(a, body):
        for half in range(2):

            def chunk(k, _, half=half):
                x = G[a, half, :, :, pl.ds(pl.multiple_of(k * 1024, 1024), 1024)].reshape(T, 1024)
                body(x, pl.multiple_of(half * HALF + k * 1024, 1024))
                return 0

            lax.fori_loop(0, HALF // 1024, chunk, 0)

    def project(a, w):
        whole(a)
        accq[...] = jnp.zeros_like(accq)
        acckv[...] = jnp.zeros_like(acckv)

        def body(x, at):
            accq[...] += mm(x, wq[pl.ds(at, 1024), :])
            acckv[:, :64] += mm(x, wkv[pl.ds(at, 1024), :])

        each_chunk(a, body)
        turned = rotate(acckv[...], kvcos_ref[...], kvsin_ref[...])
        kvt[w, j] = turned.T[:64].astype(BF16)
        for i, peer in enumerate(group):
            send(kvt.at[w, j], kvt.at[w, j], kv_s.at[w, i], kv_r.at[w, i], peer)
        for i in range(2):
            cols = slice(i * HD, (i + 1) * HD)
            q = rotate(accq[:, cols], cos_ref[...], sin_ref[...])
            qrot[:, cols] = q.astype(BF16)
            if w == 0:
                qtr[i] = q.T.astype(BF16)

    def attend(w):
        for i, peer in enumerate(group):
            from_j = [z * 0 + 2 * h + 1 - c, 2 * (1 - h) + c, 2 * (1 - h) + 1 - c][i]
            arrived(kvt.at[w, from_j], kv_s.at[w, i], kv_r.at[w, i], peer)
        kt = kvt[w, 0:2].reshape(HD, T)
        vt = kvt[w, 2:4].reshape(HD, T)
        visible = seqr_ref[...] <= seqc_ref[...]
        for i in range(2):
            cols = slice(i * HD, (i + 1) * HD)
            scores = jnp.where(visible, mm(qrot[:, cols], kt) * SCALE, NEG_FILL)
            raised = jnp.exp(scores - jnp.max(scores, axis=-1, keepdims=True))
            p = raised / jnp.sum(raised, axis=-1, keepdims=True)
            if w == 0:
                prob[i] = p
            else:
                att[:, cols] = mm_nt(p.astype(BF16), vt).astype(BF16)

    def grad_attended():
        whole(GRAD)
        accg[...] = jnp.zeros_like(accg)

        def body(x, at):
            accg[...] += mm_nt(x, wo[:, pl.ds(at, 1024)])

        each_chunk(GRAD, body)
        gab[...] = accg[...].astype(BF16)
        gatr[...] = accg[...].T.astype(BF16)

    def attention_back():
        kt = kvt[0, 0:2].reshape(HD, T)
        vt = kvt[0, 2:4].reshape(HD, T)
        key_sum = jnp.zeros((HD, T), F32)
        value_sum = jnp.zeros((HD, T), F32)
        for i in range(2):
            cols = slice(i * HD, (i + 1) * HD)
            p = prob[i]
            dp = mm(gab[:, cols], vt)
            sg = (p * (dp - jnp.sum(p * dp, axis=-1, keepdims=True)) * SCALE).astype(BF16)
            qg[:, cols] = rotate(mm_nt(sg, kt), cos_ref[...], -sin_ref[...]).astype(BF16)
            key_sum += mm(qtr[i], sg)
            value_sum += mm(gatr[cols, :], p.astype(BF16))
        kgs[0:2] = key_sum.reshape(2, 64, T).astype(BF16)
        kgs[2:4] = value_sum.reshape(2, 64, T).astype(BF16)
        for i, peer in enumerate(group):
            to_j = [2 * h + 1 - c, 2 * (1 - h) + c, 2 * (1 - h) + 1 - c][i]
            send(kgs.at[to_j], kgr.at[i], kg_s.at[i], kg_r.at[i], peer)

    def keyval_sum():
        total = kgs[j].astype(F32)
        for i, peer in enumerate(group):
            arrived(kgr.at[i], kg_s.at[i], kg_r.at[i], peer)
            total += kgr[i].astype(F32)
        total = jnp.concatenate([total, total], axis=0).T
        kvg[...] = rotate(total, kvcos_ref[...], -kvsin_ref[...]).astype(BF16)

    def spread(w, first):
        def chunk(k, _):
            at = pl.multiple_of(k * 256, 256)
            lows, highs = first(at), first(at + ENC // 2)
            for b in range(32):
                hh, zz, cc = b // 16, (b // 2) % 8, b % 2
                rows = slice(b * 8, b * 8 + 8)
                both = jnp.concatenate([lows[rows], highs[rows]], axis=0)
                rsb[w, cc, hh, zz, :, pl.ds(at, 256)] = both.astype(BF16)
            return 0

        lax.fori_loop(0, ENC // 512, chunk, 0)
        send(rsb.at[w, 1 - c], r1.at[w], rs_s.at[w, 0], rs_r.at[w, 0], sib)

    def fwd_part(at):
        return mm(att[...], woe[:, pl.ds(at, 256)])

    def back_part(at):
        return mm_nt(qg[...], qe[pl.ds(at, 256), :]) + mm_nt(kvg[:, :64], kve[pl.ds(at, 256), :])

    def reduce_x(w):
        arrived(r1.at[w], rs_s.at[w, 0], rs_r.at[w, 0], sib)
        rsb[w, c, 1 - h] = (rsb[w, c, 1 - h].astype(F32) + r1[w, 1 - h].astype(F32)).astype(BF16)
        send(rsb.at[w, c, 1 - h], r2.at[w], rs_s.at[w, 1], rs_r.at[w, 1], link["X"])

    def reduce_z(w):
        arrived(r2.at[w], rs_s.at[w, 1], rs_r.at[w, 1], link["X"])
        total = rsb[w, c, h].astype(F32) + r1[w, h].astype(F32) + r2[w].astype(F32)
        rsb[w, c, h] = total.astype(BF16)
        for k in range(1, 8):
            send(rsb.at[w, c, h, zmod(k)], r3.at[w, k - 1], rs_s.at[w, 1 + k], rs_r.at[w, 1 + k], along[k - 1])

    def reduced(w):
        total = rsb[w, c, h, z].astype(F32)
        for k in range(1, 8):
            arrived(r3.at[w, k - 1], rs_s.at[w, 1 + k], rs_r.at[w, 1 + k], along[k - 1])
            total += r3[w, k - 1].astype(F32)
        return total

    def decode_piece(encoded, i):
        rows, col = (i // 8) * 8, (i % 8) * 128
        return mm(encoded[rows : rows + 8, col : col + 128].astype(BF16), dec_bd[i * 128 : i * 128 + 128, :])

    def encode_piece(values, i):
        return mm(values, enc_bd[i * 512 : i * 512 + 512, :])

    def pass_on(w, make, out, peer):
        for i in range(8):
            both = []
            for q in (i, i + 8):
                value = make(q).astype(BF16)
                out[:, q * 512 : q * 512 + 512] = value
                both.append(encode_piece(value, q))
            pk_s[w, :, i * 128 : i * 128 + 128] = jnp.concatenate(both, axis=0).astype(BF16)
        send(pk_s.at[w], pk_r.at[w], sc_s.at[w], sc_r.at[w], peer)

    def received(w, out, peer, keep):
        arrived(pk_r.at[w], sc_s.at[w], sc_r.at[w], peer)
        got = pk_r[w].astype(F32)
        got = got * jnp.where(keep, 1.0, 0.0)
        for i in range(16):
            out[:, i * 512 : i * 512 + 512] = decode_piece(got, i).astype(BF16)

    def finish_forward():
        total = reduced(1)

        def make(i):
            return fwd_ref[:, i * 512 : i * 512 + 512].astype(F32) + decode_piece(total, i)

        pass_on(1, make, out_ref, nxt)

    def finish_back():
        total = reduced(0)
        dots = jnp.zeros((8, 1), F32)
        for i in range(16):
            cols = slice(i * 512, i * 512 + 512)
            scaled = decode_piece(total, i) * gain_ref[:, cols]
            scaled_ref[:, cols] = scaled
            dots += jnp.sum(scaled * saved_ref[:, cols].astype(F32), axis=-1, keepdims=True)
        factor = factor_ref[:, :1]
        pull = factor * factor * (dots * (1.0 / D))

        def make(i):
            cols = slice(i * 512, i * 512 + 512)
            x = saved_ref[:, cols].astype(F32)
            return grad_ref[:, cols].astype(F32) + factor * (scaled_ref[:, cols] - x * pull)

        pass_on(0, make, ig_ref, prv)

    def forward_tail():
        project(FWD, 1)
        reduce_z(0)
        attend(1)
        spread(1, fwd_part)
        reduce_x(1)
        finish_back()
        reduce_z(1)
        received(0, gs_ref, nxt, s < 7)
        finish_forward()
        received(1, act_ref, prv, s > 0)

    tasks = {
        "enc": make_enc,
        "woe": make_woe,
        "qe": make_qe,
        "projS": lambda: project(SAVED, 0),
        "attS": lambda: attend(0),
        "gatt": grad_attended,
        "bwd": attention_back,
        "kvsum": keyval_sum,
        "rsb0": lambda: spread(0, back_part),
        "rsb1": lambda: reduce_x(0),
        "fwd": forward_tail,
    }
    at = [0, 0, 0]
    for item in ORDER:
        if isinstance(item, str):
            tasks[item]()
        else:
            step(item, at[item])
            at[item] += 1
    assert at == [len(GROUPS)] * 3
    for copy in pending:
        copy.wait_send()


def on_device(
    fwd_in, saved_in, grad_in, norm_gain, query_weight, keyval_weight, out_weight, encoder, decoder, seq_pos, rope_ids
):
    def by_row(ids):
        return ids.reshape(8, 2, 16).transpose(1, 0, 2).reshape(T)

    t = lax.axis_index("tensor")
    rope = by_row(rope_ids).astype(F32)
    seq = by_row(seq_pos)
    pair_index = jnp.arange(HD // 2, dtype=F32)
    frequency = ROPE_BASE ** (-2.0 * pair_index / HD)
    angle = rope[:, None] * frequency[None, :]
    cosine, sine = jnp.cos(angle), jnp.sin(angle)
    cos_all = jnp.repeat(cosine, 2, axis=1)
    sin_all = jnp.stack([-sine, sine], axis=-1).reshape(T, HD)
    j = t % 4
    zeros = jnp.zeros((T, 64), F32)
    kv_cos = jnp.where(j == 0, cos_all[:, :64], jnp.where(j == 1, cos_all[:, 64:], 1.0))
    kv_sin = jnp.where(j == 0, sin_all[:, :64], jnp.where(j == 1, sin_all[:, 64:], 0.0))
    kv_cos = jnp.concatenate([kv_cos, zeros], axis=1)
    kv_sin = jnp.concatenate([kv_sin, zeros], axis=1)

    vmem = pl.BlockSpec(memory_space=pltpu.VMEM)
    hbm = pl.BlockSpec(memory_space=pl.ANY)
    dma = pltpu.SemaphoreType.DMA
    outs = pl.pallas_call(
        kernel,
        out_shape=[jax.ShapeDtypeStruct((8, D), BF16)] * 4,
        in_specs=[vmem] * 10 + [hbm] * 5,
        out_specs=[vmem] * 4,
        scratch_shapes=[
            pltpu.VMEM((3, 2, 16, 16, HALF), BF16),
            pltpu.VMEM((D, 256), BF16),
            pltpu.VMEM((D, 64), BF16),
            pltpu.VMEM((256, D), BF16),
            pltpu.VMEM((D, 32), F32),
            pltpu.VMEM((ENC, 128), F32),
            pltpu.VMEM((D, 128), BF16),
            pltpu.VMEM((ENC, 512), BF16),
            pltpu.VMEM((ENC, 512), BF16),
            pltpu.VMEM((256, ENC), BF16),
            pltpu.VMEM((ENC, 256), BF16),
            pltpu.VMEM((ENC, 64), BF16),
            pltpu.VMEM((3, 2, 8, HALF), F32),
            pltpu.VMEM((3, 2, 8, HALF), F32),
            pltpu.VMEM((8, 128), F32),
            pltpu.VMEM((T, 256), F32),
            pltpu.VMEM((T, 128), F32),
            pltpu.VMEM((T, 256), F32),
            pltpu.VMEM((2, 4, 64, T), BF16),
            pltpu.VMEM((T, 256), BF16),
            pltpu.VMEM((2, HD, T), BF16),
            pltpu.VMEM((T, 256), BF16),
            pltpu.VMEM((256, T), BF16),
            pltpu.VMEM((2, T, T), F32),
            pltpu.VMEM((T, 256), BF16),
            pltpu.VMEM((T, 256), BF16),
            pltpu.VMEM((T, 128), BF16),
            pltpu.VMEM((4, 64, T), BF16),
            pltpu.VMEM((3, 64, T), BF16),
            pltpu.VMEM((2, 2, 2, 8, 16, ENC // 2), BF16),
            pltpu.VMEM((2, 2, 8, 16, ENC // 2), BF16),
            pltpu.VMEM((2, 8, 16, ENC // 2), BF16),
            pltpu.VMEM((2, 7, 16, ENC // 2), BF16),
            pltpu.VMEM((2, 16, ENC // 2), BF16),
            pltpu.VMEM((2, 16, ENC // 2), BF16),
            pltpu.VMEM((8, D), F32),
            dma((5,)),
            dma((3,)),
            dma((3,)),
            dma((3, len(KEYS))),
            dma((3, len(KEYS))),
            dma((3, len(BLOCKS))),
            dma((3, len(BLOCKS))),
            dma((2, 3)),
            dma((2, 3)),
            dma((3,)),
            dma((3,)),
            dma((2, 9)),
            dma((2, 9)),
            dma((2,)),
            dma((2,)),
        ],
        compiler_params=pltpu.CompilerParams(collective_id=0, has_side_effects=True, vmem_limit_bytes=60 << 20),
        name="relay_tick",
    )(
        fwd_in[0],
        saved_in[0],
        grad_in[0],
        norm_gain,
        cos_all,
        sin_all,
        kv_cos,
        kv_sin,
        seq[:, None],
        seq[None, :],
        query_weight[0],
        keyval_weight[0],
        out_weight[0],
        encoder.reshape(D, 32),
        decoder.reshape(ENC, 128),
    )
    return tuple(o[None] for o in outs)


def solution(mesh):
    rows = P("section", "tensor", None)
    columns = P("section", None, "tensor")
    return jax.shard_map(
        on_device,
        mesh=mesh,
        in_specs=(rows, rows, rows, P("section", None), columns, columns, rows, P(), P(), P(), P()),
        out_specs=(rows, rows, rows, rows),
        check_vma=False,
    )
```

```python
import math

import jax
import jax.numpy as jnp
import numpy as np
from jax import lax
from jax.experimental import pallas as pl
from jax.experimental.pallas import tpu as pltpu
from jax.sharding import PartitionSpec as P

MESH = pl.DeviceIdType.MESH
HD = 128
D = 8192
HALF = D // 2
ENC = 2048
T = 256
EPSILON = 1e-05
ROPE_BASE = 10000.0
NEG_FILL = -1e30
SCALE = 1.0 / math.sqrt(HD)
F32 = jnp.float32
BF16 = jnp.bfloat16
GRAD, SAVED, FWD = 0, 1, 2

KEYS = [(0, 1), (0, -1), (0, 2), (0, -2), (0, 3), (0, -3), (0, 4, 0), (0, 4, 1)]
KEYS += [(1, 0), (1, 1), (1, -1), (1, 2), (1, -2), (1, 3), (1, -3), (1, 4, 0), (1, 4, 1)]
COLUMNS = [[k for k in KEYS if k[0] == 0], [k for k in KEYS if k[0] == 1]]
ORDER = [
    ("S", 0, "M", (0, 0)), ("S", 0, "P", (0, 0)), ("S", 0, "X", (0, 0)), "tables", ("S", 1, "M", (0, 0)),
    ("S", 1, "P", (0, 0)), ("S", 1, "X", (0, 0)), "enc", ("W", 0, (0, 1)), ("S", 0, "M", (0, 1)),
    ("W", 0, (0, -1)), ("S", 0, "P", (0, -1)), ("S", 0, "X", (0, 1)), ("S", 0, "X", (0, -1)),
    ("S", 2, "M", (0, 0)), ("S", 2, "P", (0, 0)), ("S", 2, "X", (0, 0)), "woe0", "woe1", ("W", 1, (0, 1)),
    ("S", 1, "M", (0, 1)), ("W", 1, (0, -1)), ("S", 1, "P", (0, -1)), ("S", 1, "X", (0, 1)), "woe2", "woe3", "qe0",
    ("W", 0, (0, 2)), ("S", 0, "M", (0, 2)), ("W", 0, (0, -2)), ("S", 0, "P", (0, -2)), ("S", 0, "X", (0, 2)),
    ("S", 0, "X", (0, -2)), "qe1", "qe2", ("W", 2, (0, 1)), ("S", 2, "M", (0, 1)), ("W", 2, (0, -1)),
    ("S", 2, "P", (0, -1)), "qe3", ("W", 1, (0, 2)), ("S", 1, "M", (0, 2)), ("W", 1, (0, -2)),
    ("S", 1, "P", (0, -2)), ("S", 1, "X", (0, 2)), ("S", 1, "X", (0, -2)), ("W", 0, (0, 3)), ("S", 0, "M", (0, 3)),
    ("W", 0, (0, -3)), ("S", 0, "P", (0, -3)), ("W", 2, (0, 2)), ("S", 2, "M", (0, 2)), ("S", 1, "X", (0, -1)),
    ("W", 0, (1, 2)), ("S", 0, "M", (1, 2)), ("W", 2, (0, -2)), ("S", 2, "P", (0, -2)), ("S", 2, "X", (0, 2)),
    ("W", 1, (0, 3)), ("S", 1, "M", (0, 3)), ("W", 1, (0, -3)), ("S", 1, "P", (0, -3)), ("W", 0, (1, -2)),
    ("S", 0, "P", (1, -2)), ("S", 2, "X", (0, -2)), ("W", 0, (0, 4, 0)), ("W", 0, (0, 4, 1)), "g00", "g01", "g02",
    ("W", 1, (1, 2)), ("S", 1, "M", (1, 2)), "g03", "gx0", ("W", 2, (0, 3)), ("S", 2, "M", (0, 3)),
    ("W", 2, (0, -3)), ("S", 2, "P", (0, -3)), ("S", 2, "X", (0, 1)), ("W", 1, (1, -2)), ("S", 1, "P", (1, -2)),
    ("W", 0, (1, 3)), ("S", 0, "M", (1, 3)), ("W", 1, (0, 4, 0)), ("W", 1, (0, 4, 1)), "s00", ("W", 0, (1, -3)),
    ("S", 0, "P", (1, -3)), ("S", 2, "X", (0, -1)), "s01", "s02", "s03", "sx0", ("W", 1, (1, 3)),
    ("S", 1, "M", (1, 3)), ("W", 2, (1, 2)), ("S", 2, "M", (1, 2)), ("W", 2, (0, 4, 0)), ("W", 2, (0, 4, 1)),
    "f00", ("W", 1, (1, -3)), ("S", 1, "P", (1, -3)), "f01", "f02", ("W", 2, (1, -2)), ("S", 2, "P", (1, -2)),
    ("W", 0, (1, 0)), ("W", 0, (1, 1)), ("W", 0, (1, -1)), ("W", 0, (1, 4, 0)), ("W", 0, (1, 4, 1)), "g10", "g11",
    "g12", "g13", "gx1", ("W", 1, (1, 0)), ("W", 1, (1, 1)), ("W", 1, (1, -1)), ("W", 1, (1, 4, 0)),
    ("W", 1, (1, 4, 1)), "s10", "s11", ("W", 2, (1, 3)), ("S", 2, "M", (1, 3)), "s12", "s13", ("W", 2, (1, -3)),
    ("S", 2, "P", (1, -3)), "sx1", "f03", "fx0", "gfin", "sfin", ("W", 2, (1, 0)), ("W", 2, (1, 1)),
    ("W", 2, (1, -1)), ("W", 2, (1, 4, 0)), ("W", 2, (1, 4, 1)), "f10", "f11", "f12", "f13", "fx1", "attS", "bwd",
    "ffin", "kvsum", "sp00", "sp01", "attF", "rx00", "rx01", "sp10", "sp11", "rx10", "rz00", "rx11", "rz01",
    "rz10", "rz11", "fin0", "fin1", "rcv0", "rcv1",
]


def mm(a, b):
    return jnp.dot(a, b, preferred_element_type=F32)


def mm_nt(a, b):
    return lax.dot_general(a, b, (((1,), (1,)), ((), ())), preferred_element_type=F32)


def rotate(x, cosine, sine):
    lane = lax.broadcasted_iota(jnp.int32, x.shape, 1)
    swapped = jnp.where(lane % 2 == 0, pltpu.roll(x, x.shape[1] - 1, 1), pltpu.roll(x, 1, 1))
    return x * cosine + swapped * sine


def kernel(
    fwd_hbm, saved_hbm, grad_hbm, gain_hbm, freq_hbm, rope_hbm, seq_hbm, wq_hbm, wkv_hbm, wo_hbm, enc_hbm, dec_hbm,
    out_hbm, act_hbm, ig_hbm, gs_hbm,
    fwd_ref, saved_ref, grad_ref, gain_ref, freq_ref, rope_ref, seq_ref, wq, wkv, wo, enc_raw, dec_raw, wqs, wkvp, wos,
    out_ref, act_ref, ig_ref, gs_ref,
    G, cos_ref, sin_ref, kvcos_ref, kvsin_ref, seqc_ref, seqr_ref, enc_bd, enc_t, dec_bd, woe, qe, kve,
    nrm, chipf, factor_ref, acc, acckv, other, got, gotkv, kvt, qrot, qtr, gab, gatr, prob, att, qg, kvg, kgs, kgr,
    rsb, r1, r2, r3, pk_s, pk_r, scaled_ref,
    wsem, osem, ws_s, ws_r, st_s, st_r, g_s, g_r, sb_s, sb_r, kv_s, kv_r, kg_s, kg_r, rs_s, rs_r, sc_s, sc_r,
):
    s = lax.axis_index("section")
    t = lax.axis_index("tensor")
    z, h, c = t // 4, (t // 2) % 2, t % 2
    j = t % 4

    def tid(zz, hh, cc):
        return (s, zz * 4 + hh * 2 + cc)

    def zmod(d):
        return lax.rem(z + d + 8, 8)

    sib = tid(z, h, 1 - c)
    link = {"M": tid(zmod(-1), h, c), "P": tid(zmod(1), h, c), "X": tid(z, 1 - h, c)}
    group = [sib, link["X"], tid(z, 1 - h, 1 - c)]
    nxt, prv = (lax.rem(s + 1, 8), t), (lax.rem(s + 7, 8), t)
    along = [tid(zmod(k), h, c) for k in range(1, 8)]

    arrays = {
        "grad": (grad_hbm, grad_ref), "saved": (saved_hbm, saved_ref), "gain": (gain_hbm, gain_ref), "fwd": (fwd_hbm, fwd_ref),
        "rope": (rope_hbm, rope_ref), "seq": (seq_hbm, seq_ref), "freq": (freq_hbm, freq_ref),
        "enc": (enc_hbm, enc_raw), "dec": (dec_hbm, dec_raw), "wo": (wo_hbm, wo), "wq": (wq_hbm, wq), "wkv": (wkv_hbm, wkv),
        "own": (wkv_hbm.at[:, pl.ds(pl.multiple_of(c * HALF, HALF), HALF)], wkvp.at[:64]),
    }
    loads = {}
    for i, (name, (src, dst)) in enumerate(arrays.items()):
        loads[name] = pltpu.make_async_copy(src, dst, wsem.at[i])
        loads[name].start()

    barrier = pltpu.get_barrier_semaphore()
    for peer in along + group + [nxt, prv]:
        pl.semaphore_signal(barrier, inc=1, device_id=peer, device_id_type=MESH)

    def put_own(a, values):
        nrm[a, 0] = values[:, :HALF]
        nrm[a, 1] = values[:, HALF:]

    def normed(ref, slot):
        x = ref[...].astype(F32)
        factor = lax.rsqrt(jnp.mean(x * x, axis=-1, keepdims=True) + EPSILON)
        if slot is not None:
            factor_ref[...] = jnp.broadcast_to(factor, factor_ref.shape)
        return x * factor * gain_ref[...]

    pending, stores = [], []

    def store(i, src, dst):
        stores.append(pltpu.make_async_copy(src, dst, osem.at[i]))
        stores[-1].start()

    def send(src, dst, ssem, rsem, peer):
        copy = pltpu.make_async_remote_copy(
            src_ref=src, dst_ref=dst, send_sem=ssem, recv_sem=rsem, device_id=peer, device_id_type=MESH
        )
        copy.start()
        pending.append(copy)

    def arrived(dst, ssem, rsem, peer):
        pltpu.make_async_remote_copy(
            src_ref=dst, dst_ref=dst, send_sem=ssem, recv_sem=rsem, device_id=peer, device_id_type=MESH
        ).wait_recv()

    def stage(a):
        send(nrm.at[a, 1 - c], chipf.at[a, c], st_s.at[a], st_r.at[a], sib)

    loads["grad"].wait()
    put_own(GRAD, grad_ref[...].astype(F32))
    pl.semaphore_wait(barrier, len(along) + len(group) + 2)
    stage(GRAD)
    loads["saved"].wait()
    loads["gain"].wait()
    put_own(SAVED, normed(saved_ref, 0))
    stage(SAVED)

    away = pl.ds(pl.multiple_of((1 - c) * HALF, HALF), HALF)
    shared = [(wo_hbm.at[:, away], wos), (wkv_hbm.at[:, away], wkvp.at[64:]), (wq_hbm.at[away, :], wqs)]
    for i, (src, dst) in enumerate(shared):
        send(src, dst, ws_s.at[i], ws_r.at[i], sib)

    def shared_in(i):
        arrived(shared[i][1], ws_s.at[i], ws_r.at[i], sib)

    def stage_last():
        loads["fwd"].wait()
        put_own(FWD, normed(fwd_ref, None))
        stage(FWD)

    def make_tables():
        loads["rope"].wait()
        loads["seq"].wait()
        loads["freq"].wait()

        def down(row):
            tall = jnp.broadcast_to(row.astype(F32), (128, T)).T
            return jnp.concatenate([tall[zz * 32 + hh * 16 :][:16] for hh in range(2) for zz in range(8)], axis=0)

        positions = down(seq_ref[...])
        seqc_ref[...] = positions
        seqr_ref[...] = positions.T[:8]
        angle = down(rope_ref[...]) * freq_ref[...]
        cosine, sine = jnp.cos(angle), jnp.sin(angle)
        sine = jnp.where(lax.broadcasted_iota(jnp.int32, sine.shape, 1) % 2 == 0, -sine, sine)
        cos_ref[...] = cosine
        sin_ref[...] = sine
        first, second = jnp.where(j == 0, 1.0, 0.0), jnp.where(j == 1, 1.0, 0.0)
        kvcos_ref[...] = first * cosine + second * pltpu.roll(cosine, 64, 1) + (1.0 - first - second)
        kvsin_ref[...] = first * sine + second * pltpu.roll(sine, 64, 1)

    def where(key):
        return (h if key[0] == 0 else 1 - h), zmod(key[1])

    def piece(a, key):
        ref = G.at[(a, *where(key))]
        if len(key) == 3:
            ref = ref.at[:, pl.ds(key[2] * (HALF // 2), HALF // 2)]
        return ref

    def form_own(a):
        if a == FWD:
            stage_last()
        arrived(chipf.at[a, 1 - c], st_s.at[a], st_r.at[a], sib)
        chipf[a, c] = nrm[a, c]
        G[a, h, z] = chipf[a].reshape(16, HALF).astype(BF16)

    def take(a, key):
        i = KEYS.index(key)
        arrived(piece(a, key), g_s.at[a, i], g_r.at[a, i], link["M"])

    def hand(a, way, key):
        column, far = (key[0], key[1] + (1 if way == "M" else -1)) if way != "X" else (1 - key[0], key[1])
        there = (column, 4, 0 if way == "M" else 1) if abs(far) == 4 else (column, far)
        i = KEYS.index(there)
        part = piece(a, key + there[2:])
        send(part, part, g_s.at[a, i], g_r.at[a, i], link[way])

    def make_enc():
        loads["enc"].wait()
        loads["dec"].wait()

        def fill(i, _):
            rows = pl.ds(i * 128, 128)
            group_row = lax.broadcasted_iota(jnp.int32, (128, 128), 0) // 32
            e, d = enc_raw[rows, :], dec_raw[rows, :]
            wide = jnp.concatenate([jnp.where(group_row == q, e, 0.0) for q in range(4)], axis=1)
            enc_t[rows, :] = wide.astype(BF16)
            enc_bd[pl.ds(i * 512, 512), :] = wide.T.astype(BF16)
            wide = jnp.concatenate([jnp.where(group_row == q, d, 0.0) for q in range(4)], axis=1)
            dec_bd[rows, :] = wide.astype(BF16)
            return 0

        lax.fori_loop(0, 16, fill, 0)

    def make_woe(part):
        if part == 0:
            loads["wo"].wait()

        def fill(i, _):
            cols = pl.ds(pl.multiple_of(i * 512, 512), 512)
            outs = pl.ds(pl.multiple_of(i * 128, 128), 128)
            woe[:, outs] = mm(wo[:, cols], enc_bd[pl.ds(i * 512, 512), :]).astype(BF16)
            return 0

        lax.fori_loop(part * 4, part * 4 + 4, fill, 0)

    def make_qe(part):
        if part == 0:
            loads["wq"].wait()
            loads["wkv"].wait()

        def fill(i, _):
            rows, outs = pl.ds(i * 512, 512), pl.ds(i * 128, 128)
            e = enc_t[outs, :]
            qe[outs, :] = mm(e, wq[rows, :]).astype(BF16)
            kve[outs, :] = mm_nt(e, wkv[:, pl.ds(pl.multiple_of(i * 512, 512), 512)]).astype(BF16)
            return 0

        lax.fori_loop(part * 4, part * 4 + 4, fill, 0)

    def rows_of(part):
        return pl.ds(pl.multiple_of((h if part == 0 else 1 - h) * 128, 128), 128)

    def contract(a, part, k):
        if part == 0 and k == 0:
            for i in [0] if a == GRAD else [1, 2]:
                if a != FWD:
                    shared_in(i)
            if a == SAVED:
                loads["own"].wait()
        rows, cols = rows_of(part), slice(k * 1024, k * 1024 + 1024)
        here = pl.ds(pl.multiple_of(c * HALF + k * 1024, 1024), 1024)
        x = G[a, h if part == 0 else 1 - h, :, :, cols].reshape(128, 1024)
        if a == GRAD:
            products = [(acc, mm_nt(x, wo[:, here])), (other, mm_nt(x, wos[:, cols]))]
        else:
            products = [(acc, mm(x, wq[here, :])), (other, mm(x, wqs[cols, :])), (acckv, mm_nt(x, wkvp[:, cols]))]
        for ref, product in products:
            if k == 0:
                ref[a, rows, :] = product
            else:
                ref[a, rows, :] += product

    def swap(a, part):
        rows = rows_of(part)
        send(other.at[a, rows], got.at[a, rows], sb_s.at[a, part, 0], sb_r.at[a, part, 0], sib)
        if a != GRAD:
            send(acckv.at[a, rows], gotkv.at[a, rows], sb_s.at[a, part, 1], sb_r.at[a, part, 1], sib)

    def swapped(a):
        for part in range(2):
            rows = rows_of(part)
            arrived(got.at[a, rows], sb_s.at[a, part, 0], sb_r.at[a, part, 0], sib)
            if a != GRAD:
                arrived(gotkv.at[a, rows], sb_s.at[a, part, 1], sb_r.at[a, part, 1], sib)

    def project(a, w):
        swapped(a)
        keyval = acckv[a] + pltpu.roll(gotkv[a], 64, 1)
        turned = rotate(keyval, kvcos_ref[...], kvsin_ref[...])
        kvt[w, j] = turned.T[:64].astype(BF16)
        for i, peer in enumerate(group):
            send(kvt.at[w, j], kvt.at[w, j], kv_s.at[w, i], kv_r.at[w, i], peer)
        for i in range(2):
            cols = slice(i * HD, (i + 1) * HD)
            q = rotate(acc[a, :, cols] + got[a, :, cols], cos_ref[...], sin_ref[...])
            qrot[w, :, cols] = q.astype(BF16)
            if w == 0:
                qtr[i] = q.T.astype(BF16)

    def attend(w):
        for i, peer in enumerate(group):
            from_j = [z * 0 + 2 * h + 1 - c, 2 * (1 - h) + c, 2 * (1 - h) + 1 - c][i]
            arrived(kvt.at[w, from_j], kv_s.at[w, i], kv_r.at[w, i], peer)
        kt = kvt[w, 0:2].reshape(HD, T)
        vt = kvt[w, 2:4].reshape(HD, T)
        visible = seqr_ref[:1, :] <= seqc_ref[:, :1]
        for i in range(2):
            cols = slice(i * HD, (i + 1) * HD)
            scores = jnp.where(visible, mm(qrot[w, :, cols], kt) * SCALE, NEG_FILL)
            raised = jnp.exp(scores - jnp.max(scores, axis=-1, keepdims=True))
            p = raised / jnp.sum(raised, axis=-1, keepdims=True)
            if w == 0:
                prob[i] = p
            else:
                att[:, cols] = mm_nt(p.astype(BF16), vt).astype(BF16)

    def grad_attended():
        swapped(GRAD)
        total = acc[GRAD] + got[GRAD]
        gab[...] = total.astype(BF16)
        gatr[...] = total.T.astype(BF16)

    def attention_back():
        kt = kvt[0, 0:2].reshape(HD, T)
        vt = kvt[0, 2:4].reshape(HD, T)
        key_sum = jnp.zeros((HD, T), F32)
        value_sum = jnp.zeros((HD, T), F32)
        for i in range(2):
            cols = slice(i * HD, (i + 1) * HD)
            p = prob[i]
            dp = mm(gab[:, cols], vt)
            sg = (p * (dp - jnp.sum(p * dp, axis=-1, keepdims=True)) * SCALE).astype(BF16)
            qg[:, cols] = rotate(mm_nt(sg, kt), cos_ref[...], -sin_ref[...]).astype(BF16)
            key_sum += mm(qtr[i], sg)
            value_sum += mm(gatr[cols, :], p.astype(BF16))
        kgs[0:2] = key_sum.reshape(2, 64, T).astype(BF16)
        kgs[2:4] = value_sum.reshape(2, 64, T).astype(BF16)
        for i, peer in enumerate(group):
            to_j = [2 * h + 1 - c, 2 * (1 - h) + c, 2 * (1 - h) + 1 - c][i]
            send(kgs.at[to_j], kgr.at[i], kg_s.at[i], kg_r.at[i], peer)

    def keyval_sum():
        total = kgs[j].astype(F32)
        for i, peer in enumerate(group):
            arrived(kgr.at[i], kg_s.at[i], kg_r.at[i], peer)
            total += kgr[i].astype(F32)
        total = jnp.concatenate([total, total], axis=0).T
        kvg[...] = rotate(total, kvcos_ref[...], -kvsin_ref[...]).astype(BF16)

    def spread(w, q, first):
        def chunk(k, _):
            at = pl.multiple_of(q * 512 + k * 256, 256)
            lows, highs = first(at), first(at + ENC // 2)
            for b in range(32):
                hh, zz, cc = b // 16, (b // 2) % 8, b % 2
                rows = slice(b * 8, b * 8 + 8)
                both = jnp.concatenate([lows[rows], highs[rows]], axis=0)
                rsb[w, q, cc, hh, zz, :, pl.ds(pl.multiple_of(k * 256, 256), 256)] = both.astype(BF16)
            return 0

        lax.fori_loop(0, 2, chunk, 0)
        send(rsb.at[w, q, 1 - c], r1.at[w, q], rs_s.at[w, q, 0], rs_r.at[w, q, 0], sib)

    def fwd_part(at):
        return mm(att[...], woe[:, pl.ds(at, 256)])

    def back_part(at):
        return mm_nt(qg[...], qe[pl.ds(at, 256), :]) + mm_nt(kvg[:, :64], kve[pl.ds(at, 256), :])

    def reduce_x(w, q):
        arrived(r1.at[w, q], rs_s.at[w, q, 0], rs_r.at[w, q, 0], sib)
        rsb[w, q, c, 1 - h] = (rsb[w, q, c, 1 - h].astype(F32) + r1[w, q, 1 - h].astype(F32)).astype(BF16)
        send(rsb.at[w, q, c, 1 - h], r2.at[w, q], rs_s.at[w, q, 1], rs_r.at[w, q, 1], link["X"])

    def reduce_z(w, q):
        arrived(r2.at[w, q], rs_s.at[w, q, 1], rs_r.at[w, q, 1], link["X"])
        total = rsb[w, q, c, h].astype(F32) + r1[w, q, h].astype(F32) + r2[w, q].astype(F32)
        rsb[w, q, c, h] = total.astype(BF16)
        for k in range(1, 8):
            sems = rs_s.at[w, q, 1 + k], rs_r.at[w, q, 1 + k]
            send(rsb.at[w, q, c, h, zmod(k)], r3.at[w, q, k - 1], *sems, along[k - 1])

    def reduced(w):
        totals = []
        for q in range(2):
            total = rsb[w, q, c, h, z].astype(F32)
            for k in range(1, 8):
                arrived(r3.at[w, q, k - 1], rs_s.at[w, q, 1 + k], rs_r.at[w, q, 1 + k], along[k - 1])
                total += r3[w, q, k - 1].astype(F32)
            totals.append(total)
        return jnp.concatenate(totals, axis=1)

    def decode_piece(encoded, i):
        rows, col = (i // 8) * 8, (i % 8) * 128
        return mm(encoded[rows : rows + 8, col : col + 128].astype(BF16), dec_bd[i * 128 : i * 128 + 128, :])

    def encode_piece(values, i):
        return mm(values, enc_bd[i * 512 : i * 512 + 512, :])

    def pass_on(w, make, out, peer):
        for i in range(8):
            both = []
            for q in (i, i + 8):
                value = make(q).astype(BF16)
                out[:, q * 512 : q * 512 + 512] = value
                both.append(encode_piece(value, q))
            pk_s[w, :, i * 128 : i * 128 + 128] = jnp.concatenate(both, axis=0).astype(BF16)
        send(pk_s.at[w], pk_r.at[w], sc_s.at[w], sc_r.at[w], peer)

    def received(w, out, peer, keep):
        arrived(pk_r.at[w], sc_s.at[w], sc_r.at[w], peer)
        got = pk_r[w].astype(F32)
        got = got * jnp.where(keep, 1.0, 0.0)
        for i in range(16):
            out[:, i * 512 : i * 512 + 512] = decode_piece(got, i).astype(BF16)

    def finish_forward():
        total = reduced(1)

        def make(i):
            return fwd_ref[:, i * 512 : i * 512 + 512].astype(F32) + decode_piece(total, i)

        pass_on(1, make, out_ref, nxt)
        store(0, out_ref, out_hbm)

    def finish_back():
        total = reduced(0)
        dots = jnp.zeros((8, 1), F32)
        for i in range(16):
            cols = slice(i * 512, i * 512 + 512)
            scaled = decode_piece(total, i) * gain_ref[:, cols]
            scaled_ref[:, cols] = scaled
            dots += jnp.sum(scaled * saved_ref[:, cols].astype(F32), axis=-1, keepdims=True)
        factor = factor_ref[:, :1]
        pull = factor * factor * (dots * (1.0 / D))

        def make(i):
            cols = slice(i * 512, i * 512 + 512)
            x = saved_ref[:, cols].astype(F32)
            return grad_ref[:, cols].astype(F32) + factor * (scaled_ref[:, cols] - x * pull)

        pass_on(0, make, ig_ref, prv)
        store(2, ig_ref, ig_hbm)

    def get_grad():
        received(0, gs_ref, nxt, s < 7)
        store(3, gs_ref, gs_hbm)

    def get_act():
        received(1, act_ref, prv, s > 0)
        store(1, act_ref, act_hbm)

    tasks = {
        "tables": make_tables,
        "enc": make_enc,
        "sfin": lambda: project(SAVED, 0),
        "attS": lambda: attend(0),
        "gfin": grad_attended,
        "bwd": attention_back,
        "kvsum": keyval_sum,
        "ffin": lambda: project(FWD, 1),
        "attF": lambda: attend(1),
        "fin0": finish_back,
        "fin1": finish_forward,
        "rcv0": get_grad,
        "rcv1": get_act,
    }
    for i in range(4):
        tasks[f"woe{i}"] = lambda i=i: make_woe(i)
        tasks[f"qe{i}"] = lambda i=i: make_qe(i)
    for a, name in enumerate("gsf"):
        for part in range(2):
            tasks[f"{name}x{part}"] = lambda a=a, part=part: swap(a, part)
            for k in range(4):
                tasks[f"{name}{part}{k}"] = lambda a=a, part=part, k=k: contract(a, part, k)
    for w, first in enumerate((back_part, fwd_part)):
        for q in range(2):
            tasks[f"sp{w}{q}"] = lambda w=w, q=q, first=first: spread(w, q, first)
            tasks[f"rx{w}{q}"] = lambda w=w, q=q: reduce_x(w, q)
            tasks[f"rz{w}{q}"] = lambda w=w, q=q: reduce_z(w, q)
    formed = set()
    for item in ORDER:
        if isinstance(item, str):
            tasks[item]()
        elif item[0] == "W":
            take(*item[1:])
        else:
            if item[1] not in formed:
                formed.add(item[1])
                form_own(item[1])
            hand(*item[1:])
    for copy in pending:
        copy.wait_send()
    for copy in stores:
        copy.wait()


def hand_over(*refs):
    for i in range(4):
        refs[4 + i][...] = refs[i][...]


def on_device(
    fwd_in, saved_in, grad_in, norm_gain, query_weight, keyval_weight, out_weight, encoder, decoder, seq_pos, rope_ids
):
    frequency = np.repeat(ROPE_BASE ** (-2.0 * np.arange(HD // 2) / HD), 2)[None].astype(np.float32)
    operands = [
        fwd_in[0],
        saved_in[0],
        grad_in[0],
        norm_gain,
        jnp.asarray(frequency),
        rope_ids[None],
        seq_pos[None],
        query_weight[0],
        keyval_weight[0].T,
        out_weight[0],
        encoder.transpose(0, 2, 1).reshape(ENC, 128),
        decoder.reshape(ENC, 128),
    ]
    hbm = pl.BlockSpec(memory_space=pl.ANY)
    vmem = pl.BlockSpec(memory_space=pltpu.VMEM)
    dma = pltpu.SemaphoreType.DMA
    shapes = [jax.ShapeDtypeStruct((8, D), BF16)] * 4
    outs = pl.pallas_call(
        kernel,
        out_shape=shapes,
        in_specs=[hbm] * len(operands),
        out_specs=[hbm] * 4,
        scratch_shapes=[pltpu.VMEM(x.shape, x.dtype) for x in operands]
        + [
            pltpu.VMEM((D // 2, 256), BF16),
            pltpu.VMEM((128, HALF), BF16),
            pltpu.VMEM((256, HALF), BF16),
        ]
        + [pltpu.VMEM((8, D), BF16)] * 4
        + [
            pltpu.VMEM((3, 2, 8, 16, HALF), BF16),
            pltpu.VMEM((T, HD), F32),
            pltpu.VMEM((T, HD), F32),
            pltpu.VMEM((T, HD), F32),
            pltpu.VMEM((T, HD), F32),
            pltpu.VMEM((T, HD), F32),
            pltpu.VMEM((8, T), F32),
            pltpu.VMEM((D, 128), BF16),
            pltpu.VMEM((ENC, 512), BF16),
            pltpu.VMEM((ENC, 512), BF16),
            pltpu.VMEM((256, ENC), BF16),
            pltpu.VMEM((ENC, 256), BF16),
            pltpu.VMEM((ENC, 64), BF16),
            pltpu.VMEM((3, 2, 8, HALF), F32),
            pltpu.VMEM((3, 2, 8, HALF), F32),
            pltpu.VMEM((8, 128), F32),
            pltpu.VMEM((3, T, 256), F32),
            pltpu.VMEM((3, T, 128), F32),
            pltpu.VMEM((3, T, 256), F32),
            pltpu.VMEM((3, T, 256), F32),
            pltpu.VMEM((3, T, 128), F32),
            pltpu.VMEM((2, 4, 64, T), BF16),
            pltpu.VMEM((2, T, 256), BF16),
            pltpu.VMEM((2, HD, T), BF16),
            pltpu.VMEM((T, 256), BF16),
            pltpu.VMEM((256, T), BF16),
            pltpu.VMEM((2, T, T), F32),
            pltpu.VMEM((T, 256), BF16),
            pltpu.VMEM((T, 256), BF16),
            pltpu.VMEM((T, 128), BF16),
            pltpu.VMEM((4, 64, T), BF16),
            pltpu.VMEM((3, 64, T), BF16),
            pltpu.VMEM((2, 2, 2, 2, 8, 16, ENC // 4), BF16),
            pltpu.VMEM((2, 2, 2, 8, 16, ENC // 4), BF16),
            pltpu.VMEM((2, 2, 8, 16, ENC // 4), BF16),
            pltpu.VMEM((2, 2, 7, 16, ENC // 4), BF16),
            pltpu.VMEM((2, 16, ENC // 2), BF16),
            pltpu.VMEM((2, 16, ENC // 2), BF16),
            pltpu.VMEM((8, D), F32),
            dma((len(operands) + 1,)),
            dma((4,)),
            dma((3,)),
            dma((3,)),
            dma((3,)),
            dma((3,)),
            dma((3, len(KEYS))),
            dma((3, len(KEYS))),
            dma((3, 2, 2)),
            dma((3, 2, 2)),
            dma((2, 3)),
            dma((2, 3)),
            dma((3,)),
            dma((3,)),
            dma((2, 2, 9)),
            dma((2, 2, 9)),
            dma((2,)),
            dma((2,)),
        ],
        compiler_params=pltpu.CompilerParams(collective_id=0, has_side_effects=True, vmem_limit_bytes=60 << 20),
        name="relay_tick",
    )(*operands)
    outs = pl.pallas_call(
        hand_over,
        out_shape=shapes,
        in_specs=[vmem] * 4,
        out_specs=[vmem] * 4,
        name="hand_over",
    )(*outs)
    return tuple(o[None] for o in outs)


def solution(mesh):
    rows = P("section", "tensor", None)
    columns = P("section", None, "tensor")
    return jax.shard_map(
        on_device,
        mesh=mesh,
        in_specs=(rows, rows, rows, P("section", None), columns, columns, rows, P(), P(), P(), P()),
        out_specs=(rows, rows, rows, rows),
        check_vma=False,
    )
```

```python
import math

import jax
import jax.numpy as jnp
import numpy as np
from jax import lax
from jax.experimental import pallas as pl
from jax.experimental.pallas import tpu as pltpu
from jax.sharding import PartitionSpec as P

MESH = pl.DeviceIdType.MESH
HD = 128
D = 8192
HALF = D // 2
ENC = 2048
T = 256
EPSILON = 1e-05
ROPE_BASE = 10000.0
NEG_FILL = -1e30
SCALE = 1.0 / math.sqrt(HD)
F32 = jnp.float32
BF16 = jnp.bfloat16
SAVED, GRAD, FWD = 0, 1, 2
Z_FIRST = ((0, 1),)

KEYS = [(0, 1), (0, -1), (0, 2), (0, -2), (0, 3), (0, -3), (0, 4, 0), (0, 4, 1)]
KEYS += [(1, 0), (1, 1), (1, -1), (1, 2), (1, -2), (1, 3), (1, -3), (1, 4, 0), (1, 4, 1)]
COLUMNS = [[k for k in KEYS if k[0] == 0], [k for k in KEYS if k[0] == 1]]
ORDER = [
    ("S", 0, "M", (0, 0)), ("S", 0, "P", (0, 0)), ("S", 0, "X", (0, 0)), "tables", ("S", 1, "M", (0, 0)),
    ("S", 1, "P", (0, 0)), "enc", ("S", 1, "X", (0, 0)), "woe0", "woe1", ("W", 0, (0, 1)), ("S", 0, "M", (0, 1)),
    ("W", 0, (0, -1)), ("S", 0, "P", (0, -1)), "woe2", ("S", 0, "X", (0, 1)), "woe3", ("W", 1, (0, 1)),
    ("S", 1, "M", (0, 1)), ("W", 1, (0, -1)), ("S", 1, "P", (0, -1)), "qe0", "qe1", ("S", 0, "X", (0, -1)), "qe2",
    ("W", 0, (0, 2)), ("S", 0, "M", (0, 2)), ("W", 0, (0, -2)), ("S", 0, "P", (0, -2)), ("S", 0, "X", (0, 2)),
    "qe3", ("S", 2, "M", (0, 0)), ("S", 2, "P", (0, 0)), "maps", ("S", 0, "X", (0, -2)), "own", ("W", 1, (0, 2)),
    ("S", 1, "M", (0, 2)), ("W", 1, (0, -2)), ("S", 1, "P", (0, -2)), ("S", 1, "X", (0, 2)), ("W", 0, (0, 3)),
    ("S", 0, "M", (0, 3)), ("W", 0, (0, -3)), ("S", 0, "P", (0, -3)), ("W", 0, (1, 2)), ("S", 0, "M", (1, 2)),
    ("S", 1, "X", (0, -2)), ("W", 2, (0, -1)), ("S", 2, "P", (0, -1)), ("W", 2, (0, 1)), ("S", 2, "M", (0, 1)),
    ("W", 0, (1, -2)), ("S", 0, "P", (1, -2)), ("S", 1, "X", (0, 1)), ("W", 0, (0, 4, 0)), ("W", 0, (0, 4, 1)),
    "s00", "s01", "s02", ("W", 1, (0, 3)), ("S", 1, "M", (0, 3)), ("W", 1, (0, -3)), ("S", 1, "P", (0, -3)), "s03",
    "sk0", "sx0", ("W", 1, (1, 2)), ("S", 1, "M", (1, 2)), ("W", 1, (1, -2)), ("S", 1, "P", (1, -2)),
    ("W", 2, (0, -2)), ("S", 2, "X", (0, -2)), ("W", 0, (1, 3)), ("S", 0, "M", (1, 3)), ("S", 2, "P", (0, -2)),
    ("W", 2, (0, 2)), ("S", 2, "X", (0, 2)), ("S", 2, "M", (0, 2)), ("W", 1, (0, 4, 0)), ("W", 1, (0, 4, 1)),
    "g00", "g01", "g02", ("W", 0, (1, -3)), ("S", 0, "P", (1, -3)), "g03", "gx0", ("W", 1, (1, 3)),
    ("S", 1, "M", (1, 3)), ("W", 1, (1, -3)), ("S", 1, "P", (1, -3)), ("S", 1, "X", (0, -1)), ("W", 2, (1, -2)),
    ("S", 2, "P", (1, -2)), ("S", 2, "X", (0, 0)), ("W", 2, (1, 2)), ("S", 2, "M", (1, 2)), ("W", 2, (0, -3)),
    ("S", 2, "P", (0, -3)), ("W", 2, (0, 3)), ("S", 2, "M", (0, 3)), ("W", 0, (1, 0)), ("W", 0, (1, 1)),
    ("W", 0, (1, -1)), ("W", 0, (1, 4, 0)), ("W", 0, (1, 4, 1)), "s10", "s11", "s12", ("S", 2, "X", (0, 1)),
    ("W", 1, (1, 0)), ("W", 1, (1, 1)), ("W", 1, (1, -1)), ("W", 1, (1, 4, 0)), ("W", 1, (1, 4, 1)), "g10", "g11",
    "g12", "g13", "gx1", "s13", "sk1", ("W", 2, (1, 3)), ("S", 2, "M", (1, 3)), ("W", 2, (1, -3)),
    ("S", 2, "P", (1, -3)), "sx1", ("S", 2, "X", (0, -1)), ("W", 2, (0, 4, 0)), ("W", 2, (0, 4, 1)), "f00", "f01",
    "f02", "f03", "fk0", "fx0", "gfin", "sfin", "attS", "bwd", ("W", 2, (1, 0)), ("W", 2, (1, 1)),
    ("W", 2, (1, -1)), ("W", 2, (1, 4, 0)), ("W", 2, (1, 4, 1)), "f10", "f11", "f12", "f13", "fk1", "fx1", "kvsum",
    "sp01", "sp00", "ffin", "rz01", "attF", "rx00", "sp11", "sp10", "rx11", "rx10", "rz00", "rx01", "rz11", "rz10",
    "fin0", "rcv0", "fin1", "rcv1",
]


def mm(a, b):
    return jnp.dot(a, b, preferred_element_type=F32)


def mm_nt(a, b):
    return lax.dot_general(a, b, (((1,), (1,)), ((), ())), preferred_element_type=F32)


def rotate(x, cosine, sine):
    lane = lax.broadcasted_iota(jnp.int32, x.shape, 1)
    swapped = jnp.where(lane % 2 == 0, pltpu.roll(x, x.shape[1] - 1, 1), pltpu.roll(x, 1, 1))
    return x * cosine + swapped * sine


def kernel(
    fwd_hbm, saved_hbm, grad_hbm, gain_hbm, freq_hbm, rope_hbm, seq_hbm, wq_hbm, wkv_hbm, wo_hbm, enc_hbm, dec_hbm,
    out_hbm, act_hbm, ig_hbm, gs_hbm,
    fwd_ref, saved_ref, grad_ref, gain_ref, freq_ref, rope_ref, seq_ref, wq, wkv, wo, enc_raw, dec_raw, wqs, wos,
    out_ref, act_ref, ig_ref, gs_ref,
    G, cos_ref, sin_ref, kvcos_ref, kvsin_ref, seqc_ref, seqr_ref, enc_bd, enc_t, dec_bd, woe, qe, kve, de, dge, enc_fwd, enc_saved, enc_grad, pull_ref,
    nrm, chipf, factor_ref, acc, acckv, other, got, kvp, kvt, qrot, qtr, gab, gatr, prob, att, qg, kvg, kgs, kgr,
    rsb, r1, r2, r3, rz, rz1, rz3, rz2, pk_s, pk_r,
    wsem, osem, ws_s, ws_r, st_s, st_r, g_s, g_r, sb_s, sb_r, kv_s, kv_r, kg_s, kg_r, rs_s, rs_r, sc_s, sc_r,
):
    s = lax.axis_index("section")
    t = lax.axis_index("tensor")
    z, h, c = t // 4, (t // 2) % 2, t % 2

    def tid(zz, hh, cc):
        return (s, zz * 4 + hh * 2 + cc)

    def zmod(d):
        return lax.rem(z + d + 8, 8)

    sib = tid(z, h, 1 - c)
    link = {"M": tid(zmod(-1), h, c), "P": tid(zmod(1), h, c), "X": tid(z, 1 - h, c)}
    group = [sib, link["X"], tid(z, 1 - h, 1 - c)]
    nxt, prv = (lax.rem(s + 1, 8), t), (lax.rem(s + 7, 8), t)
    along = [tid(zmod(k), h, c) for k in range(1, 8)]

    arrays = {
        "saved": (saved_hbm, saved_ref), "gain": (gain_hbm, gain_ref), "grad": (grad_hbm, grad_ref), "fwd": (fwd_hbm, fwd_ref),
        "rope": (rope_hbm, rope_ref), "seq": (seq_hbm, seq_ref), "freq": (freq_hbm, freq_ref),
        "enc": (enc_hbm, enc_raw), "dec": (dec_hbm, dec_raw), "wo": (wo_hbm, wo), "wq": (wq_hbm, wq), "wkv": (wkv_hbm, wkv.at[c]),
    }
    loads = {}
    for i, (name, (src, dst)) in enumerate(arrays.items()):
        loads[name] = pltpu.make_async_copy(src, dst, wsem.at[i])
        loads[name].start()

    barrier = pltpu.get_barrier_semaphore()
    for peer in along + group + [nxt, prv]:
        pl.semaphore_signal(barrier, inc=1, device_id=peer, device_id_type=MESH)

    def put_own(a, values):
        nrm[a, 0] = values[:, :HALF]
        nrm[a, 1] = values[:, HALF:]

    def normed(ref, slot):
        x = ref[...].astype(F32)
        factor = lax.rsqrt(jnp.mean(x * x, axis=-1, keepdims=True) + EPSILON)
        if slot is not None:
            factor_ref[...] = jnp.broadcast_to(factor, factor_ref.shape)
        return x * factor * gain_ref[...]

    pending, stores = [], []

    def store(i, src, dst):
        stores.append(pltpu.make_async_copy(src, dst, osem.at[i]))
        stores[-1].start()

    def send(src, dst, ssem, rsem, peer):
        copy = pltpu.make_async_remote_copy(
            src_ref=src, dst_ref=dst, send_sem=ssem, recv_sem=rsem, device_id=peer, device_id_type=MESH
        )
        copy.start()
        pending.append(copy)

    def arrived(dst, ssem, rsem, peer):
        pltpu.make_async_remote_copy(
            src_ref=dst, dst_ref=dst, send_sem=ssem, recv_sem=rsem, device_id=peer, device_id_type=MESH
        ).wait_recv()

    def stage(a):
        send(nrm.at[a, 1 - c], chipf.at[a, c], st_s.at[a], st_r.at[a], sib)

    loads["saved"].wait()
    loads["gain"].wait()
    put_own(SAVED, normed(saved_ref, 0))
    pl.semaphore_wait(barrier, len(along) + len(group) + 2)
    stage(SAVED)
    loads["grad"].wait()
    put_own(GRAD, grad_ref[...].astype(F32))
    stage(GRAD)
    loads["fwd"].wait()
    put_own(FWD, normed(fwd_ref, None))
    stage(FWD)

    away = pl.ds(pl.multiple_of((1 - c) * HALF, HALF), HALF)
    shared = [(wq_hbm.at[away, :], wqs), (wkv_hbm, wkv.at[c]), (wo_hbm.at[:, away], wos)]
    for i, (src, dst) in enumerate(shared):
        send(src, dst, ws_s.at[i], ws_r.at[i], sib)

    ready = set()

    def need(*names):
        for name in names:
            if name in ready:
                continue
            ready.add(name)
            if isinstance(name, int):
                dst = wkv.at[1 - c] if name == 1 else shared[name][1]
                arrived(dst, ws_s.at[name], ws_r.at[name], sib)
            else:
                loads[name].wait()

    def make_tables():
        need("rope", "seq", "freq")

        def down(row):
            tall = jnp.broadcast_to(row.astype(F32), (128, T)).T
            return jnp.concatenate([tall[zz * 32 + hh * 16 :][:16] for hh in range(2) for zz in range(8)], axis=0)

        positions = down(seq_ref[...])
        seqc_ref[...] = positions
        seqr_ref[...] = positions.T[:8]
        angle = down(rope_ref[...]) * freq_ref[...]
        cosine, sine = jnp.cos(angle), jnp.sin(angle)
        sine = jnp.where(lax.broadcasted_iota(jnp.int32, sine.shape, 1) % 2 == 0, -sine, sine)
        cos_ref[...] = cosine
        sin_ref[...] = sine
        is_key = jnp.where(h == 0, 1.0, 0.0)
        kvcos_ref[...] = is_key * cosine + (1.0 - is_key)
        kvsin_ref[...] = is_key * sine

    def where(key):
        return (h if key[0] == 0 else 1 - h), zmod(key[1])

    def piece(a, key):
        ref = G.at[(a, *where(key))]
        if len(key) == 3:
            ref = ref.at[:, pl.ds(key[2] * (HALF // 2), HALF // 2)]
        return ref

    def form_own(a):
        arrived(chipf.at[a, 1 - c], st_s.at[a], st_r.at[a], sib)
        chipf[a, c] = nrm[a, c]
        G[a, h, z] = chipf[a].reshape(16, HALF).astype(BF16)

    def take(a, key):
        i = KEYS.index(key)
        arrived(piece(a, key), g_s.at[a, i], g_r.at[a, i], link["M"])

    def hand(a, way, key):
        column, far = (key[0], key[1] + (1 if way == "M" else -1)) if way != "X" else (1 - key[0], key[1])
        there = (column, 4, 0 if way == "M" else 1) if abs(far) == 4 else (column, far)
        i = KEYS.index(there)
        part = piece(a, key + there[2:])
        send(part, part, g_s.at[a, i], g_r.at[a, i], link[way])

    def make_enc():
        need("enc", "dec")

        def fill(i, _):
            rows = pl.ds(i * 128, 128)
            group_row = lax.broadcasted_iota(jnp.int32, (128, 128), 0) // 32
            e, d = enc_raw[rows, :], dec_raw[rows, :]
            wide = jnp.concatenate([jnp.where(group_row == q, e, 0.0) for q in range(4)], axis=1)
            enc_t[rows, :] = wide.astype(BF16)
            enc_bd[pl.ds(i * 512, 512), :] = wide.T.astype(BF16)
            wide = jnp.concatenate([jnp.where(group_row == q, d, 0.0) for q in range(4)], axis=1)
            dec_bd[rows, :] = wide.astype(BF16)
            return 0

        lax.fori_loop(0, 16, fill, 0)

    def make_woe(part):
        need("wo")

        def fill(i, _):
            cols = pl.ds(pl.multiple_of(i * 512, 512), 512)
            outs = pl.ds(pl.multiple_of(i * 128, 128), 128)
            woe[:, outs] = mm(wo[:, cols], enc_bd[pl.ds(i * 512, 512), :]).astype(BF16)
            return 0

        lax.fori_loop(part * 4, part * 4 + 4, fill, 0)

    def make_qe(part):
        need("wq", "wkv", 1)

        def fill(i, _):
            rows, outs = pl.ds(i * 512, 512), pl.ds(i * 128, 128)
            e = enc_t[outs, :]
            qe[outs, :] = mm(e, wq[rows, :]).astype(BF16)
            kve[outs, :] = mm_nt(e, wkv[:, :, pl.ds(pl.multiple_of(i * 512, 512), 512)].reshape(128, 512)).astype(BF16)
            return 0

        lax.fori_loop(part * 4, part * 4 + 4, fill, 0)

    def rows_of(part):
        return pl.ds(pl.multiple_of((h if part == 0 else 1 - h) * 128, 128), 128)

    def contract(a, part, k):
        need(*(("wo", 2) if a == GRAD else ("wq", "wkv", 0, 1)))
        rows, cols = rows_of(part), slice(k * 1024, k * 1024 + 1024)
        here = pl.ds(pl.multiple_of(c * HALF + k * 1024, 1024), 1024)
        x = G[a, h if part == 0 else 1 - h, :, :, cols].reshape(128, 1024)
        if a == GRAD:
            products = [(acc, mm_nt(x, wo[:, here])), (other, mm_nt(x, wos[:, cols]))]
        else:
            products = [(acc, mm(x, wq[here, :])), (other, mm(x, wqs[cols, :])), (acckv, mm_nt(x, wkv[:, :, here].reshape(128, 1024)))]
        for ref, product in products:
            if k == 0:
                ref[a, rows, :] = product
            else:
                ref[a, rows, :] += product

    def swap(a, part):
        rows = rows_of(part)
        send(other.at[a, rows], got.at[a, rows], sb_s.at[a, part], sb_r.at[a, part], sib)

    def swapped(a):
        for part in range(2):
            rows = rows_of(part)
            arrived(got.at[a, rows], sb_s.at[a, part], sb_r.at[a, part], sib)

    def keyvals(a, w, part):
        rows, col = rows_of(part), h if part == 0 else 1 - h
        turned = rotate(acckv[a, rows, :], kvcos_ref[rows, :], kvsin_ref[rows, :])
        mine = kvp.at[w, h, c, col]
        mine[...] = turned.T.astype(BF16)
        for i, peer in enumerate(group):
            send(mine, mine, kv_s.at[w, part, i], kv_r.at[w, part, i], peer)

    def keyvals_in(w):
        for part in range(2):
            col = h if part == 0 else 1 - h
            for i, (hh, cc) in enumerate([(h, 1 - c), (1 - h, c), (1 - h, 1 - c)]):
                arrived(kvp.at[w, hh, cc, col], kv_s.at[w, part, i], kv_r.at[w, part, i], group[i])
        for hh in range(2):
            for col in range(2):
                total = kvp[w, hh, 0, col].astype(F32) + kvp[w, hh, 1, col].astype(F32)
                kvt[w, hh, :, col * 128 : col * 128 + 128] = total.astype(BF16)

    def project(a, w):
        swapped(a)
        for i in range(2):
            cols = slice(i * HD, (i + 1) * HD)
            q = rotate(acc[a, :, cols] + got[a, :, cols], cos_ref[...], sin_ref[...])
            qrot[w, :, cols] = q.astype(BF16)
            if w == 0:
                qtr[i] = q.T.astype(BF16)

    def attend(w):
        keyvals_in(w)
        kt, vt = kvt[w, 0], kvt[w, 1]
        visible = seqr_ref[:1, :] <= seqc_ref[:, :1]
        for i in range(2):
            cols = slice(i * HD, (i + 1) * HD)
            scores = jnp.where(visible, mm(qrot[w, :, cols], kt) * SCALE, NEG_FILL)
            raised = jnp.exp(scores - jnp.max(scores, axis=-1, keepdims=True))
            p = raised / jnp.sum(raised, axis=-1, keepdims=True)
            if w == 0:
                prob[i] = p
            else:
                att[:, cols] = mm_nt(p.astype(BF16), vt).astype(BF16)

    def grad_attended():
        swapped(GRAD)
        total = acc[GRAD] + got[GRAD]
        gab[...] = total.astype(BF16)
        gatr[...] = total.T.astype(BF16)

    def attention_back():
        kt, vt = kvt[0, 0], kvt[0, 1]
        key_sum = jnp.zeros((HD, T), F32)
        value_sum = jnp.zeros((HD, T), F32)
        for i in range(2):
            cols = slice(i * HD, (i + 1) * HD)
            p = prob[i]
            dp = mm(gab[:, cols], vt)
            sg = (p * (dp - jnp.sum(p * dp, axis=-1, keepdims=True)) * SCALE).astype(BF16)
            qg[:, cols] = rotate(mm_nt(sg, kt), cos_ref[...], -sin_ref[...]).astype(BF16)
            key_sum += mm(qtr[i], sg)
            value_sum += mm(gatr[cols, :], p.astype(BF16))
        kgs[0] = key_sum.astype(BF16)
        kgs[1] = value_sum.astype(BF16)
        send(kgs.at[1 - h], kgr, kg_s, kg_r, link["X"])

    def keyval_sum():
        arrived(kgr, kg_s, kg_r, link["X"])
        total = kgs[h].astype(F32) + kgr[...].astype(F32)
        kvg[...] = rotate(total.T, kvcos_ref[...], -kvsin_ref[...]).astype(BF16)

    def spread(w, q, first):
        def chunk(k, _):
            at = pl.multiple_of(q * 512 + k * 256, 256)
            lows, highs = first(at), first(at + ENC // 2)
            cols = pl.ds(pl.multiple_of(k * 256, 256), 256)
            for b in range(32):
                hh, zz, cc = b // 16, (b // 2) % 8, b % 2
                rows = slice(b * 8, b * 8 + 8)
                both = jnp.concatenate([lows[rows], highs[rows]], axis=0).astype(BF16)
                if (w, q) in Z_FIRST:
                    rz[w, q, cc, zz, hh, :, cols] = both
                else:
                    rsb[w, q, cc, hh, zz, :, cols] = both
            return 0

        lax.fori_loop(0, 2, chunk, 0)
        src, dst = (rz, rz1) if (w, q) in Z_FIRST else (rsb, r1)
        send(src.at[w, q, 1 - c], dst.at[w, q], rs_s.at[w, q, 0], rs_r.at[w, q, 0], sib)

    def fwd_part(at):
        return mm(att[...], woe[:, pl.ds(at, 256)])

    def back_part(at):
        return mm_nt(qg[...], qe[pl.ds(at, 256), :]) + mm_nt(kvg[...], kve[pl.ds(at, 256), :])

    def from_core(w, q):
        arrived((rz1 if (w, q) in Z_FIRST else r1).at[w, q], rs_s.at[w, q, 0], rs_r.at[w, q, 0], sib)

    def along_z(w, q, slots, total):
        for k in range(1, 8):
            arrived(slots.at[w, q, k - 1], rs_s.at[w, q, 1 + k], rs_r.at[w, q, 1 + k], along[k - 1])
            total += slots[w, q, k - 1].astype(F32)
        return total

    def reduce_x(w, q):
        sems = rs_s.at[w, q, 1], rs_r.at[w, q, 1]
        if (w, q) in Z_FIRST:
            rz[w, q, c, z] = along_z(w, q, rz3, rz[w, q, c, z].astype(F32)).astype(BF16)
            send(rz.at[w, q, c, z, 1 - h], rz2.at[w, q], *sems, link["X"])
        else:
            from_core(w, q)
            rsb[w, q, c, 1 - h] = (rsb[w, q, c, 1 - h].astype(F32) + r1[w, q, 1 - h].astype(F32)).astype(BF16)
            send(rsb.at[w, q, c, 1 - h], r2.at[w, q], *sems, link["X"])

    def reduce_z(w, q):
        if (w, q) in Z_FIRST:
            from_core(w, q)
            rz[w, q, c] = (rz[w, q, c].astype(F32) + rz1[w, q].astype(F32)).astype(BF16)
        else:
            arrived(r2.at[w, q], rs_s.at[w, q, 1], rs_r.at[w, q, 1], link["X"])
            total = rsb[w, q, c, h].astype(F32) + r1[w, q, h].astype(F32) + r2[w, q].astype(F32)
            rsb[w, q, c, h] = total.astype(BF16)
        for k in (4, 3, 5, 2, 6, 1, 7):
            sems = rs_s.at[w, q, 1 + k], rs_r.at[w, q, 1 + k]
            if (w, q) in Z_FIRST:
                send(rz.at[w, q, c, zmod(k)], rz3.at[w, q, k - 1], *sems, along[k - 1])
            else:
                send(rsb.at[w, q, c, h, zmod(k)], r3.at[w, q, k - 1], *sems, along[k - 1])

    def reduced(w):
        totals = []
        for q in range(2):
            if (w, q) in Z_FIRST:
                arrived(rz2.at[w, q], rs_s.at[w, q, 1], rs_r.at[w, q, 1], link["X"])
                totals.append(rz[w, q, c, z, h].astype(F32) + rz2[w, q].astype(F32))
            else:
                totals.append(along_z(w, q, r3, rsb[w, q, c, h, z].astype(F32)))
        return jnp.concatenate(totals, axis=1)

    def part_of(i):
        return slice((i // 8) * 8, (i // 8) * 8 + 8), slice((i % 8) * 128, (i % 8) * 128 + 128)

    def wide(i):
        return slice(i * 512, i * 512 + 512)

    def each_group(make):
        return [jnp.concatenate([make(i), make(i + 8)], axis=0) for i in range(8)]

    def decode_piece(encoded, i):
        return mm(encoded[part_of(i)].astype(BF16), dec_bd[i * 128 : i * 128 + 128, :])

    def make_maps():
        def fill(i, _):
            rows, cols = pl.ds(i * 128, 128), pl.ds(pl.multiple_of(i * 512, 512), 512)
            d, e = dec_bd[rows, :], enc_bd[pl.ds(i * 512, 512), :]
            de[rows, :] = mm(d, e).astype(BF16)
            dge[rows, :] = mm((d.astype(F32) * gain_ref[:, cols]).astype(BF16), e).astype(BF16)
            return 0

        lax.fori_loop(0, 16, fill, 0)

    def make_encoded():
        def encode(ref):
            return each_group(lambda i: mm(ref[:, wide(i)], enc_bd[i * 512 : i * 512 + 512, :]))

        def pull(i):
            x = saved_ref[:, wide(i)].astype(F32) * gain_ref[:, wide(i)]
            return mm_nt(x.astype(BF16), dec_bd[i * 128 : i * 128 + 128, :])

        for i, parts in enumerate(zip(encode(fwd_ref), encode(saved_ref), encode(grad_ref), each_group(pull))):
            for ref, value in zip((enc_fwd, enc_saved, enc_grad, pull_ref), parts):
                ref[:, i * 128 : i * 128 + 128] = value

    def pack(w, values, peer):
        pk_s[w] = values.astype(BF16)
        send(pk_s.at[w], pk_r.at[w], sc_s.at[w], sc_r.at[w], peer)

    def mapped(total, table):
        parts = each_group(lambda i: mm(total[part_of(i)].astype(BF16), table[i * 128 : i * 128 + 128, :]))
        return jnp.concatenate(parts, axis=1)

    def received(w, out, peer, keep):
        arrived(pk_r.at[w], sc_s.at[w], sc_r.at[w], peer)
        got = pk_r[w].astype(F32)
        got = got * jnp.where(keep, 1.0, 0.0)
        for i in range(16):
            out[:, wide(i)] = decode_piece(got, i).astype(BF16)

    def finish_forward():
        total = reduced(1)
        pack(1, enc_fwd[...] + mapped(total, de), nxt)
        for i in range(16):
            out_ref[:, wide(i)] = (fwd_ref[:, wide(i)].astype(F32) + decode_piece(total, i)).astype(BF16)
        store(0, out_ref, out_hbm)

    def finish_back():
        total = reduced(0)
        dots = jnp.sum(total * pull_ref[...], axis=-1, keepdims=True)
        factor = factor_ref[:, :1]
        pull = factor * factor * ((dots[:8] + dots[8:]) * (1.0 / D))
        both = jnp.concatenate([factor, factor], axis=0), jnp.concatenate([pull, pull], axis=0)
        pack(0, enc_grad[...] + both[0] * (mapped(total, dge) - both[1] * enc_saved[...]), prv)
        for i in range(16):
            x = saved_ref[:, wide(i)].astype(F32)
            scaled = decode_piece(total, i) * gain_ref[:, wide(i)]
            value = grad_ref[:, wide(i)].astype(F32) + factor * (scaled - x * pull)
            ig_ref[:, wide(i)] = value.astype(BF16)
        store(2, ig_ref, ig_hbm)

    def get_grad():
        received(0, gs_ref, nxt, s < 7)
        store(3, gs_ref, gs_hbm)

    def get_act():
        received(1, act_ref, prv, s > 0)
        store(1, act_ref, act_hbm)

    tasks = {
        "tables": make_tables,
        "enc": make_enc,
        "maps": make_maps,
        "own": make_encoded,
        "sfin": lambda: project(SAVED, 0),
        "attS": lambda: attend(0),
        "gfin": grad_attended,
        "bwd": attention_back,
        "kvsum": keyval_sum,
        "ffin": lambda: project(FWD, 1),
        "attF": lambda: attend(1),
        "fin0": finish_back,
        "fin1": finish_forward,
        "rcv0": get_grad,
        "rcv1": get_act,
    }
    for i in range(4):
        tasks[f"woe{i}"] = lambda i=i: make_woe(i)
        tasks[f"qe{i}"] = lambda i=i: make_qe(i)
    for a, name in ((SAVED, "s"), (GRAD, "g"), (FWD, "f")):
        for part in range(2):
            tasks[f"{name}x{part}"] = lambda a=a, part=part: swap(a, part)
            for k in range(4):
                tasks[f"{name}{part}{k}"] = lambda a=a, part=part, k=k: contract(a, part, k)
    for name, a, w in (("s", SAVED, 0), ("f", FWD, 1)):
        for part in range(2):
            tasks[f"{name}k{part}"] = lambda a=a, w=w, part=part: keyvals(a, w, part)
    for w, first in enumerate((back_part, fwd_part)):
        for q in range(2):
            tasks[f"sp{w}{q}"] = lambda w=w, q=q, first=first: spread(w, q, first)
            tasks[f"rx{w}{q}"] = lambda w=w, q=q: reduce_x(w, q)
            tasks[f"rz{w}{q}"] = lambda w=w, q=q: reduce_z(w, q)
    formed = set()
    for item in ORDER:
        if isinstance(item, str):
            tasks[item]()
        elif item[0] == "W":
            take(*item[1:])
        else:
            if item[1] not in formed:
                formed.add(item[1])
                form_own(item[1])
            hand(*item[1:])
    for copy in pending:
        copy.wait_send()
    for copy in stores:
        copy.wait()


def hand_over(*refs):
    for i in range(4):
        refs[4 + i][...] = refs[i][...]


def on_device(
    fwd_in, saved_in, grad_in, norm_gain, query_weight, keyval_weight, out_weight, encoder, decoder, seq_pos, rope_ids
):
    frequency = np.repeat(ROPE_BASE ** (-2.0 * np.arange(HD // 2) / HD), 2)[None].astype(np.float32)
    operands = [
        fwd_in[0],
        saved_in[0],
        grad_in[0],
        norm_gain,
        jnp.asarray(frequency),
        rope_ids[None],
        seq_pos[None],
        query_weight[0],
        keyval_weight[0].T,
        out_weight[0],
        encoder.transpose(0, 2, 1).reshape(ENC, 128),
        decoder.reshape(ENC, 128),
    ]
    hbm = pl.BlockSpec(memory_space=pl.ANY)
    vmem = pl.BlockSpec(memory_space=pltpu.VMEM)
    dma = pltpu.SemaphoreType.DMA
    shapes = [jax.ShapeDtypeStruct((8, D), BF16)] * 4
    outs = pl.pallas_call(
        kernel,
        out_shape=shapes,
        in_specs=[hbm] * len(operands),
        out_specs=[hbm] * 4,
        scratch_shapes=[pltpu.VMEM((2, *x.shape) if x.shape[0] == 64 else x.shape, x.dtype) for x in operands]
        + [
            pltpu.VMEM((D // 2, 256), BF16),
            pltpu.VMEM((256, HALF), BF16),
        ]
        + [pltpu.VMEM((8, D), BF16)] * 4
        + [
            pltpu.VMEM((3, 2, 8, 16, HALF), BF16),
            pltpu.VMEM((T, HD), F32),
            pltpu.VMEM((T, HD), F32),
            pltpu.VMEM((T, HD), F32),
            pltpu.VMEM((T, HD), F32),
            pltpu.VMEM((T, HD), F32),
            pltpu.VMEM((8, T), F32),
            pltpu.VMEM((D, 128), BF16),
            pltpu.VMEM((ENC, 512), BF16),
            pltpu.VMEM((ENC, 512), BF16),
            pltpu.VMEM((256, ENC), BF16),
            pltpu.VMEM((ENC, 256), BF16),
            pltpu.VMEM((ENC, 128), BF16),
            pltpu.VMEM((ENC, 128), BF16),
            pltpu.VMEM((ENC, 128), BF16),
            pltpu.VMEM((16, ENC // 2), F32),
            pltpu.VMEM((16, ENC // 2), F32),
            pltpu.VMEM((16, ENC // 2), F32),
            pltpu.VMEM((16, ENC // 2), F32),
            pltpu.VMEM((3, 2, 8, HALF), F32),
            pltpu.VMEM((3, 2, 8, HALF), F32),
            pltpu.VMEM((8, 128), F32),
            pltpu.VMEM((3, T, 256), F32),
            pltpu.VMEM((3, T, 128), F32),
            pltpu.VMEM((3, T, 256), F32),
            pltpu.VMEM((3, T, 256), F32),
            pltpu.VMEM((2, 2, 2, 2, HD, 128), BF16),
            pltpu.VMEM((2, 2, HD, T), BF16),
            pltpu.VMEM((2, T, 256), BF16),
            pltpu.VMEM((2, HD, T), BF16),
            pltpu.VMEM((T, 256), BF16),
            pltpu.VMEM((256, T), BF16),
            pltpu.VMEM((2, T, T), F32),
            pltpu.VMEM((T, 256), BF16),
            pltpu.VMEM((T, 256), BF16),
            pltpu.VMEM((T, 128), BF16),
            pltpu.VMEM((2, HD, T), BF16),
            pltpu.VMEM((HD, T), BF16),
            pltpu.VMEM((2, 2, 2, 2, 8, 16, ENC // 4), BF16),
            pltpu.VMEM((2, 2, 2, 8, 16, ENC // 4), BF16),
            pltpu.VMEM((2, 2, 8, 16, ENC // 4), BF16),
            pltpu.VMEM((2, 2, 7, 16, ENC // 4), BF16),
            pltpu.VMEM((2, 2, 2, 8, 2, 16, ENC // 4), BF16),
            pltpu.VMEM((2, 2, 8, 2, 16, ENC // 4), BF16),
            pltpu.VMEM((2, 2, 7, 2, 16, ENC // 4), BF16),
            pltpu.VMEM((2, 2, 16, ENC // 4), BF16),
            pltpu.VMEM((2, 16, ENC // 2), BF16),
            pltpu.VMEM((2, 16, ENC // 2), BF16),
            dma((len(operands),)),
            dma((4,)),
            dma((3,)),
            dma((3,)),
            dma((3,)),
            dma((3,)),
            dma((3, len(KEYS))),
            dma((3, len(KEYS))),
            dma((3, 2)),
            dma((3, 2)),
            dma((2, 2, 3)),
            dma((2, 2, 3)),
            dma(()),
            dma(()),
            dma((2, 2, 9)),
            dma((2, 2, 9)),
            dma((2,)),
            dma((2,)),
        ],
        compiler_params=pltpu.CompilerParams(collective_id=0, has_side_effects=True, vmem_limit_bytes=60 << 20),
        name="relay_tick",
    )(*operands)
    outs = pl.pallas_call(
        hand_over,
        out_shape=shapes,
        in_specs=[vmem] * 4,
        out_specs=[vmem] * 4,
        name="hand_over",
    )(*outs)
    return tuple(o[None] for o in outs)


def solution(mesh):
    rows = P("section", "tensor", None)
    columns = P("section", None, "tensor")
    return jax.shard_map(
        on_device,
        mesh=mesh,
        in_specs=(rows, rows, rows, P("section", None), columns, columns, rows, P(), P(), P(), P()),
        out_specs=(rows, rows, rows, rows),
        check_vma=False,
    )
```

```python
import math

import jax
import jax.numpy as jnp
import numpy as np
from jax import lax
from jax.experimental import pallas as pl
from jax.experimental.pallas import tpu as pltpu
from jax.sharding import PartitionSpec as P

MESH = pl.DeviceIdType.MESH
HD = 128
D = 8192
HALF = D // 2
ENC = 2048
T = 256
EPSILON = 1e-05
ROPE_BASE = 10000.0
NEG_FILL = -1e30
SCALE = 1.0 / math.sqrt(HD)
F32 = jnp.float32
BF16 = jnp.bfloat16
SAVED, GRAD, FWD = 0, 1, 2
Z_FIRST = ((1, 1),)

KEYS = [(0, 1), (0, -1), (0, 2), (0, -2), (0, 3), (0, -3), (0, 4, 0), (0, 4, 1)]
KEYS += [(1, 0), (1, 1), (1, -1), (1, 2), (1, -2), (1, 3), (1, -3), (1, 4, 0), (1, 4, 1)]
COLUMNS = [[k for k in KEYS if k[0] == 0], [k for k in KEYS if k[0] == 1]]
ORDER = [
    ("S", 0, "M", (0, 0)), ("S", 0, "P", (0, 0)), ("S", 0, "X", (0, 0)), "tables", ("S", 1, "M", (0, 0)),
    ("S", 1, "P", (0, 0)), ("S", 1, "X", (0, 0)), "enc", ("S", 2, "M", (0, 0)), ("S", 2, "P", (0, 0)),
    ("S", 2, "X", (0, 0)), "woe0", ("W", 0, (0, 1)), ("S", 0, "M", (0, 1)), ("W", 0, (0, -1)),
    ("S", 0, "P", (0, -1)), ("S", 0, "X", (0, 1)), "woe1", "woe2", ("S", 0, "X", (0, -1)), "woe3",
    ("W", 1, (0, 1)), ("S", 1, "M", (0, 1)), ("W", 1, (0, -1)), ("S", 1, "P", (0, -1)), "qe0", "qe1",
    ("S", 1, "X", (0, 1)), ("W", 2, (0, 1)), ("S", 2, "M", (0, 1)), ("W", 2, (0, -1)), ("S", 2, "P", (0, -1)),
    "qe2", "qe3", "maps", ("W", 0, (0, 2)), ("S", 0, "M", (0, 2)), ("W", 0, (0, -2)), ("S", 0, "P", (0, -2)),
    ("S", 0, "X", (0, 2)), "own", ("S", 0, "X", (0, -2)), ("W", 1, (0, 2)), ("S", 1, "M", (0, 2)),
    ("W", 1, (0, -2)), ("S", 1, "P", (0, -2)), ("S", 1, "X", (0, 2)), ("W", 2, (0, 2)), ("S", 2, "M", (0, 2)),
    ("W", 2, (0, -2)), ("S", 2, "P", (0, -2)), ("S", 1, "X", (0, -2)), ("W", 0, (0, 3)), ("S", 0, "M", (0, 3)),
    ("W", 0, (0, -3)), ("S", 0, "P", (0, -3)), ("W", 0, (1, 2)), ("S", 0, "M", (1, 2)), ("S", 2, "X", (0, 2)),
    ("W", 1, (0, -3)), ("S", 1, "P", (0, -3)), ("W", 0, (1, -2)), ("S", 0, "P", (1, -2)), ("W", 1, (0, 3)),
    ("S", 1, "M", (0, 3)), ("S", 2, "X", (0, -2)), ("W", 2, (0, 3)), ("S", 2, "M", (0, 3)), ("W", 2, (0, -3)),
    ("S", 2, "P", (0, -3)), ("W", 1, (1, 2)), ("S", 1, "M", (1, 2)), ("W", 0, (0, 4, 0)), ("W", 0, (0, 4, 1)),
    "s00", "s01", ("S", 1, "X", (0, -1)), "s02", ("W", 1, (1, -2)), ("S", 1, "P", (1, -2)), "s03", "sk0", "sx0",
    ("W", 0, (1, 3)), ("S", 0, "M", (1, 3)), ("W", 1, (0, 4, 0)), ("W", 1, (0, 4, 1)), "g00", ("W", 0, (1, -3)),
    ("S", 0, "P", (1, -3)), ("W", 2, (1, 2)), ("S", 2, "M", (1, 2)), "g01", ("S", 2, "X", (0, 1)), "g02", "g03",
    "gx0", ("W", 2, (0, 4, 0)), ("W", 2, (0, 4, 1)), "f00", "f01", ("W", 2, (1, -2)), ("S", 2, "P", (1, -2)),
    "f02", ("S", 2, "X", (0, -1)), "f03", ("W", 1, (1, 3)), ("S", 1, "M", (1, 3)), ("W", 1, (1, -3)),
    ("S", 1, "P", (1, -3)), "fk0", "fx0", ("W", 0, (1, 0)), ("W", 0, (1, 1)), ("W", 0, (1, -1)),
    ("W", 0, (1, 4, 0)), ("W", 0, (1, 4, 1)), "s10", "s11", "s12", "s13", "sk1", "sx1", ("W", 2, (1, 3)),
    ("S", 2, "M", (1, 3)), ("W", 2, (1, -3)), ("S", 2, "P", (1, -3)), ("W", 1, (1, 0)), ("W", 1, (1, 1)),
    ("W", 1, (1, -1)), ("W", 1, (1, 4, 0)), ("W", 1, (1, 4, 1)), "g10", "g11", "g12", "g13", "gx1", "sfin",
    ("W", 2, (1, 0)), ("W", 2, (1, 1)), ("W", 2, (1, -1)), ("W", 2, (1, 4, 0)), ("W", 2, (1, 4, 1)), "f10", "f11",
    "f12", "f13", "fk1", "fx1", "gfin", "attS", "bwd", "ffin", "attF", "sp11", "sp10", "kvsum", "sp01", "sp00",
    "rz11", "rx10", "rx01", "rx00", "rz10", "rx11", "rz01", "rz00", "fin1", "rcv1", "fin0", "rcv0",
]


def mm(a, b):
    return jnp.dot(a, b, preferred_element_type=F32)


def mm_nt(a, b):
    return lax.dot_general(a, b, (((1,), (1,)), ((), ())), preferred_element_type=F32)


def rotate(x, cosine, sine):
    lane = lax.broadcasted_iota(jnp.int32, x.shape, 1)
    swapped = jnp.where(lane % 2 == 0, pltpu.roll(x, x.shape[1] - 1, 1), pltpu.roll(x, 1, 1))
    return x * cosine + swapped * sine


def kernel(
    fwd_hbm, saved_hbm, grad_hbm, gain_hbm, freq_hbm, rope_hbm, seq_hbm, wq_hbm, wkv_hbm, wo_hbm, enc_hbm, dec_hbm,
    out_hbm, act_hbm, ig_hbm, gs_hbm,
    fwd_ref, saved_ref, grad_ref, gain_ref, freq_ref, rope_ref, seq_ref, wq, wkv, wo, enc_raw, dec_raw, wqs, wos,
    out_ref, act_ref, ig_ref, gs_ref,
    G, cos_ref, sin_ref, kvcos_ref, kvsin_ref, seqc_ref, seqr_ref, enc_bd, enc_t, dec_bd, woe, qe, kve, de, dge, enc_fwd, enc_saved, enc_grad, pull_ref,
    nrm, chipf, factor_ref, acc, acckv, other, got, kvp, kvt, qrot, qtr, gab, gatr, prob, att, qg, kvg, kgs, kgr,
    rsb, r1, r2, r3, rz, rz1, rz3, rz2, pk_s, pk_r,
    wsem, osem, ws_s, ws_r, st_s, st_r, g_s, g_r, sb_s, sb_r, kv_s, kv_r, kg_s, kg_r, rs_s, rs_r, sc_s, sc_r,
):
    s = lax.axis_index("section")
    t = lax.axis_index("tensor")
    z, h, c = t // 4, (t // 2) % 2, t % 2

    def tid(zz, hh, cc):
        return (s, zz * 4 + hh * 2 + cc)

    def zmod(d):
        return lax.rem(z + d + 8, 8)

    sib = tid(z, h, 1 - c)
    link = {"M": tid(zmod(-1), h, c), "P": tid(zmod(1), h, c), "X": tid(z, 1 - h, c)}
    group = [sib, link["X"], tid(z, 1 - h, 1 - c)]
    nxt, prv = (lax.rem(s + 1, 8), t), (lax.rem(s + 7, 8), t)
    along = [tid(zmod(k), h, c) for k in range(1, 8)]

    arrays = {
        "saved": (saved_hbm, saved_ref), "gain": (gain_hbm, gain_ref), "grad": (grad_hbm, grad_ref), "fwd": (fwd_hbm, fwd_ref),
        "rope": (rope_hbm, rope_ref), "seq": (seq_hbm, seq_ref), "freq": (freq_hbm, freq_ref),
        "enc": (enc_hbm, enc_raw), "dec": (dec_hbm, dec_raw), "wo": (wo_hbm, wo), "wq": (wq_hbm, wq), "wkv": (wkv_hbm, wkv.at[c]),
    }
    loads = {}
    for i, (name, (src, dst)) in enumerate(arrays.items()):
        loads[name] = pltpu.make_async_copy(src, dst, wsem.at[i])
        if i < 4:
            loads[name].start()

    barrier = pltpu.get_barrier_semaphore()
    for peer in along + group + [nxt, prv]:
        pl.semaphore_signal(barrier, inc=1, device_id=peer, device_id_type=MESH)

    def put_own(a, values):
        nrm[a, 0] = values[:, :HALF]
        nrm[a, 1] = values[:, HALF:]

    def normed(ref, slot):
        x = ref[...].astype(F32)
        factor = lax.rsqrt(jnp.mean(x * x, axis=-1, keepdims=True) + EPSILON)
        if slot is not None:
            factor_ref[...] = jnp.broadcast_to(factor, factor_ref.shape)
        return x * factor * gain_ref[...]

    pending, stores = [], []

    def store(i, src, dst):
        stores.append(pltpu.make_async_copy(src, dst, osem.at[i]))
        stores[-1].start()

    def send(src, dst, ssem, rsem, peer):
        copy = pltpu.make_async_remote_copy(
            src_ref=src, dst_ref=dst, send_sem=ssem, recv_sem=rsem, device_id=peer, device_id_type=MESH
        )
        copy.start()
        pending.append(copy)

    def drain(keep):
        while len(pending) > keep:
            pending.pop(0).wait_send()

    def arrived(dst, ssem, rsem, peer):
        pltpu.make_async_remote_copy(
            src_ref=dst, dst_ref=dst, send_sem=ssem, recv_sem=rsem, device_id=peer, device_id_type=MESH
        ).wait_recv()

    def stage(a):
        send(nrm.at[a, 1 - c], chipf.at[a, c], st_s.at[a], st_r.at[a], sib)

    loads["saved"].wait()
    loads["gain"].wait()
    put_own(SAVED, normed(saved_ref, 0))
    pl.semaphore_wait(barrier, len(along) + len(group) + 2)
    stage(SAVED)
    for name in list(arrays)[4:]:
        loads[name].start()
    loads["grad"].wait()
    put_own(GRAD, grad_ref[...].astype(F32))
    stage(GRAD)
    loads["fwd"].wait()
    put_own(FWD, normed(fwd_ref, None))
    stage(FWD)

    away = pl.ds(pl.multiple_of((1 - c) * HALF, HALF), HALF)
    shared = [(wq_hbm.at[away, :], wqs), (wkv_hbm, wkv.at[c]), (wo_hbm.at[:, away], wos)]
    for i, (src, dst) in enumerate(shared):
        send(src, dst, ws_s.at[i], ws_r.at[i], sib)

    ready = set()

    def need(*names):
        for name in names:
            if name in ready:
                continue
            ready.add(name)
            if isinstance(name, int):
                dst = wkv.at[1 - c] if name == 1 else shared[name][1]
                arrived(dst, ws_s.at[name], ws_r.at[name], sib)
            else:
                loads[name].wait()

    def make_tables():
        need("rope", "seq", "freq")

        def down(row):
            tall = jnp.broadcast_to(row.astype(F32), (128, T)).T
            return jnp.concatenate([tall[zz * 32 + hh * 16 :][:16] for hh in range(2) for zz in range(8)], axis=0)

        positions = down(seq_ref[...])
        seqc_ref[...] = positions
        seqr_ref[...] = positions.T[:8]
        angle = down(rope_ref[...]) * freq_ref[...]
        cosine, sine = jnp.cos(angle), jnp.sin(angle)
        sine = jnp.where(lax.broadcasted_iota(jnp.int32, sine.shape, 1) % 2 == 0, -sine, sine)
        cos_ref[...] = cosine
        sin_ref[...] = sine
        is_key = jnp.where(h == 0, 1.0, 0.0)
        kvcos_ref[...] = is_key * cosine + (1.0 - is_key)
        kvsin_ref[...] = is_key * sine

    def where(key):
        return (h if key[0] == 0 else 1 - h), zmod(key[1])

    def piece(a, key):
        ref = G.at[(a, *where(key))]
        if len(key) == 3:
            ref = ref.at[:, pl.ds(key[2] * (HALF // 2), HALF // 2)]
        return ref

    def form_own(a):
        arrived(chipf.at[a, 1 - c], st_s.at[a], st_r.at[a], sib)
        chipf[a, c] = nrm[a, c]
        G[a, h, z] = chipf[a].reshape(16, HALF).astype(BF16)

    def take(a, key):
        i = KEYS.index(key)
        arrived(piece(a, key), g_s.at[a, i], g_r.at[a, i], link["M"])

    def hand(a, way, key):
        column, far = (key[0], key[1] + (1 if way == "M" else -1)) if way != "X" else (1 - key[0], key[1])
        there = (column, 4, 0 if way == "M" else 1) if abs(far) == 4 else (column, far)
        i = KEYS.index(there)
        part = piece(a, key + there[2:])
        send(part, part, g_s.at[a, i], g_r.at[a, i], link[way])

    def make_enc():
        need("enc", "dec")

        def fill(i, _):
            rows = pl.ds(i * 128, 128)
            group_row = lax.broadcasted_iota(jnp.int32, (128, 128), 0) // 32
            e, d = enc_raw[rows, :], dec_raw[rows, :]
            wide = jnp.concatenate([jnp.where(group_row == q, e, 0.0) for q in range(4)], axis=1)
            enc_t[rows, :] = wide.astype(BF16)
            enc_bd[pl.ds(i * 512, 512), :] = wide.T.astype(BF16)
            wide = jnp.concatenate([jnp.where(group_row == q, d, 0.0) for q in range(4)], axis=1)
            dec_bd[rows, :] = wide.astype(BF16)
            return 0

        lax.fori_loop(0, 16, fill, 0)

    def make_woe(part):
        need("wo")

        def fill(i, _):
            cols = pl.ds(pl.multiple_of(i * 512, 512), 512)
            outs = pl.ds(pl.multiple_of(i * 128, 128), 128)
            woe[:, outs] = mm(wo[:, cols], enc_bd[pl.ds(i * 512, 512), :]).astype(BF16)
            return 0

        lax.fori_loop(part * 4, part * 4 + 4, fill, 0)

    def make_qe(part):
        need("wq", "wkv", 1)

        def fill(i, _):
            rows, outs = pl.ds(i * 512, 512), pl.ds(i * 128, 128)
            e = enc_t[outs, :]
            qe[outs, :] = mm(e, wq[rows, :]).astype(BF16)
            kve[outs, :] = mm_nt(e, wkv[:, :, pl.ds(pl.multiple_of(i * 512, 512), 512)].reshape(128, 512)).astype(BF16)
            return 0

        lax.fori_loop(part * 4, part * 4 + 4, fill, 0)

    def rows_of(part):
        return pl.ds(pl.multiple_of((h if part == 0 else 1 - h) * 128, 128), 128)

    def contract(a, part, k):
        need(*(("wo", 2) if a == GRAD else ("wq", "wkv", 0, 1)))
        rows, cols = rows_of(part), slice(k * 1024, k * 1024 + 1024)
        here = pl.ds(pl.multiple_of(c * HALF + k * 1024, 1024), 1024)
        x = G[a, h if part == 0 else 1 - h, :, :, cols].reshape(128, 1024)
        if a == GRAD:
            products = [(acc, mm_nt(x, wo[:, here])), (other, mm_nt(x, wos[:, cols]))]
        else:
            products = [(acc, mm(x, wq[here, :])), (other, mm(x, wqs[cols, :])), (acckv, mm_nt(x, wkv[:, :, here].reshape(128, 1024)))]
        for ref, product in products:
            if k == 0:
                ref[a, rows, :] = product
            else:
                ref[a, rows, :] += product

    def swap(a, part):
        rows = rows_of(part)
        send(other.at[a, rows], got.at[a, rows], sb_s.at[a, part], sb_r.at[a, part], sib)

    def swapped(a):
        for part in range(2):
            rows = rows_of(part)
            arrived(got.at[a, rows], sb_s.at[a, part], sb_r.at[a, part], sib)

    def keyvals(a, w, part):
        rows, col = rows_of(part), h if part == 0 else 1 - h
        turned = rotate(acckv[a, rows, :], kvcos_ref[rows, :], kvsin_ref[rows, :])
        mine = kvp.at[w, h, c, col]
        mine[...] = turned.T.astype(BF16)
        for i, peer in enumerate(group):
            send(mine, mine, kv_s.at[w, part, i], kv_r.at[w, part, i], peer)

    def keyvals_in(w):
        for part in range(2):
            col = h if part == 0 else 1 - h
            for i, (hh, cc) in enumerate([(h, 1 - c), (1 - h, c), (1 - h, 1 - c)]):
                arrived(kvp.at[w, hh, cc, col], kv_s.at[w, part, i], kv_r.at[w, part, i], group[i])
        for hh in range(2):
            for col in range(2):
                total = kvp[w, hh, 0, col].astype(F32) + kvp[w, hh, 1, col].astype(F32)
                kvt[w, hh, :, col * 128 : col * 128 + 128] = total.astype(BF16)

    def project(a, w):
        swapped(a)
        for i in range(2):
            cols = slice(i * HD, (i + 1) * HD)
            q = rotate(acc[a, :, cols] + got[a, :, cols], cos_ref[...], sin_ref[...])
            qrot[w, :, cols] = q.astype(BF16)
            if w == 0:
                qtr[i] = q.T.astype(BF16)

    def attend(w):
        keyvals_in(w)
        kt, vt = kvt[w, 0], kvt[w, 1]
        visible = seqr_ref[:1, :] <= seqc_ref[:, :1]
        for i in range(2):
            cols = slice(i * HD, (i + 1) * HD)
            scores = jnp.where(visible, mm(qrot[w, :, cols], kt) * SCALE, NEG_FILL)
            raised = jnp.exp(scores - jnp.max(scores, axis=-1, keepdims=True))
            p = raised / jnp.sum(raised, axis=-1, keepdims=True)
            if w == 0:
                prob[i] = p
            else:
                att[:, cols] = mm_nt(p.astype(BF16), vt).astype(BF16)

    def grad_attended():
        swapped(GRAD)
        total = acc[GRAD] + got[GRAD]
        gab[...] = total.astype(BF16)
        gatr[...] = total.T.astype(BF16)

    def attention_back():
        kt, vt = kvt[0, 0], kvt[0, 1]
        key_sum = jnp.zeros((HD, T), F32)
        value_sum = jnp.zeros((HD, T), F32)
        for i in range(2):
            cols = slice(i * HD, (i + 1) * HD)
            p = prob[i]
            dp = mm(gab[:, cols], vt)
            sg = (p * (dp - jnp.sum(p * dp, axis=-1, keepdims=True)) * SCALE).astype(BF16)
            qg[:, cols] = rotate(mm_nt(sg, kt), cos_ref[...], -sin_ref[...]).astype(BF16)
            key_sum += mm(qtr[i], sg)
            value_sum += mm(gatr[cols, :], p.astype(BF16))
        kgs[0] = key_sum.astype(BF16)
        kgs[1] = value_sum.astype(BF16)
        send(kgs.at[1 - h], kgr, kg_s, kg_r, link["X"])

    def keyval_sum():
        arrived(kgr, kg_s, kg_r, link["X"])
        total = kgs[h].astype(F32) + kgr[...].astype(F32)
        kvg[...] = rotate(total.T, kvcos_ref[...], -kvsin_ref[...]).astype(BF16)

    def spread(w, q, first):
        def chunk(k, _):
            at = pl.multiple_of(q * 512 + k * 256, 256)
            lows, highs = first(at), first(at + ENC // 2)
            cols = pl.ds(pl.multiple_of(k * 256, 256), 256)
            for b in range(32):
                hh, zz, cc = b // 16, (b // 2) % 8, b % 2
                rows = slice(b * 8, b * 8 + 8)
                both = jnp.concatenate([lows[rows], highs[rows]], axis=0).astype(BF16)
                if (w, q) in Z_FIRST:
                    rz[w, q, cc, zz, hh, :, cols] = both
                else:
                    rsb[w, q, cc, hh, zz, :, cols] = both
            return 0

        lax.fori_loop(0, 2, chunk, 0)
        src, dst = (rz, rz1) if (w, q) in Z_FIRST else (rsb, r1)
        send(src.at[w, q, 1 - c], dst.at[w, q], rs_s.at[w, q, 0], rs_r.at[w, q, 0], sib)

    def fwd_part(at):
        return mm(att[...], woe[:, pl.ds(at, 256)])

    def back_part(at):
        return mm_nt(qg[...], qe[pl.ds(at, 256), :]) + mm_nt(kvg[...], kve[pl.ds(at, 256), :])

    def from_core(w, q):
        arrived((rz1 if (w, q) in Z_FIRST else r1).at[w, q], rs_s.at[w, q, 0], rs_r.at[w, q, 0], sib)

    def along_z(w, q, slots, total):
        for k in range(1, 8):
            arrived(slots.at[w, q, k - 1], rs_s.at[w, q, 1 + k], rs_r.at[w, q, 1 + k], along[k - 1])
            total += slots[w, q, k - 1].astype(F32)
        return total

    def reduce_x(w, q):
        sems = rs_s.at[w, q, 1], rs_r.at[w, q, 1]
        if (w, q) in Z_FIRST:
            rz[w, q, c, z] = along_z(w, q, rz3, rz[w, q, c, z].astype(F32)).astype(BF16)
            send(rz.at[w, q, c, z, 1 - h], rz2.at[w, q], *sems, link["X"])
        else:
            from_core(w, q)
            rsb[w, q, c, 1 - h] = (rsb[w, q, c, 1 - h].astype(F32) + r1[w, q, 1 - h].astype(F32)).astype(BF16)
            send(rsb.at[w, q, c, 1 - h], r2.at[w, q], *sems, link["X"])

    def reduce_z(w, q):
        if (w, q) in Z_FIRST:
            from_core(w, q)
            rz[w, q, c] = (rz[w, q, c].astype(F32) + rz1[w, q].astype(F32)).astype(BF16)
        else:
            arrived(r2.at[w, q], rs_s.at[w, q, 1], rs_r.at[w, q, 1], link["X"])
            total = rsb[w, q, c, h].astype(F32) + r1[w, q, h].astype(F32) + r2[w, q].astype(F32)
            rsb[w, q, c, h] = total.astype(BF16)
        for k in (4, 3, 5, 2, 6, 1, 7):
            sems = rs_s.at[w, q, 1 + k], rs_r.at[w, q, 1 + k]
            if (w, q) in Z_FIRST:
                send(rz.at[w, q, c, zmod(k)], rz3.at[w, q, k - 1], *sems, along[k - 1])
            else:
                send(rsb.at[w, q, c, h, zmod(k)], r3.at[w, q, k - 1], *sems, along[k - 1])

    def reduced(w):
        totals = []
        for q in range(2):
            if (w, q) in Z_FIRST:
                arrived(rz2.at[w, q], rs_s.at[w, q, 1], rs_r.at[w, q, 1], link["X"])
                totals.append(rz[w, q, c, z, h].astype(F32) + rz2[w, q].astype(F32))
            else:
                totals.append(along_z(w, q, r3, rsb[w, q, c, h, z].astype(F32)))
        return jnp.concatenate(totals, axis=1)

    def part_of(i):
        return slice((i // 8) * 8, (i // 8) * 8 + 8), slice((i % 8) * 128, (i % 8) * 128 + 128)

    def wide(i):
        return slice(i * 512, i * 512 + 512)

    def each_group(make):
        return [jnp.concatenate([make(i), make(i + 8)], axis=0) for i in range(8)]

    def decode_piece(encoded, i):
        return mm(encoded[part_of(i)].astype(BF16), dec_bd[i * 128 : i * 128 + 128, :])

    def make_maps():
        def fill(i, _):
            rows, cols = pl.ds(i * 128, 128), pl.ds(pl.multiple_of(i * 512, 512), 512)
            d, e = dec_bd[rows, :], enc_bd[pl.ds(i * 512, 512), :]
            de[rows, :] = mm(d, e).astype(BF16)
            dge[rows, :] = mm((d.astype(F32) * gain_ref[:, cols]).astype(BF16), e).astype(BF16)
            return 0

        lax.fori_loop(0, 16, fill, 0)

    def make_encoded():
        def encode(ref):
            return each_group(lambda i: mm(ref[:, wide(i)], enc_bd[i * 512 : i * 512 + 512, :]))

        def pull(i):
            x = saved_ref[:, wide(i)].astype(F32) * gain_ref[:, wide(i)]
            return mm_nt(x.astype(BF16), dec_bd[i * 128 : i * 128 + 128, :])

        for i, parts in enumerate(zip(encode(fwd_ref), encode(saved_ref), encode(grad_ref), each_group(pull))):
            for ref, value in zip((enc_fwd, enc_saved, enc_grad, pull_ref), parts):
                ref[:, i * 128 : i * 128 + 128] = value

    def pack(w, values, peer):
        pk_s[w] = values.astype(BF16)
        send(pk_s.at[w], pk_r.at[w], sc_s.at[w], sc_r.at[w], peer)

    def mapped(total, table):
        parts = each_group(lambda i: mm(total[part_of(i)].astype(BF16), table[i * 128 : i * 128 + 128, :]))
        return jnp.concatenate(parts, axis=1)

    def received(w, out, peer, keep):
        arrived(pk_r.at[w], sc_s.at[w], sc_r.at[w], peer)
        got = pk_r[w].astype(F32)
        got = got * jnp.where(keep, 1.0, 0.0)
        for i in range(16):
            out[:, wide(i)] = decode_piece(got, i).astype(BF16)

    def finish_forward():
        drain(40)
        total = reduced(1)
        pack(1, enc_fwd[...] + mapped(total, de), nxt)
        for i in range(16):
            out_ref[:, wide(i)] = (fwd_ref[:, wide(i)].astype(F32) + decode_piece(total, i)).astype(BF16)
        store(0, out_ref, out_hbm)

    def finish_back():
        drain(40)
        total = reduced(0)
        dots = jnp.sum(total * pull_ref[...], axis=-1, keepdims=True)
        factor = factor_ref[:, :1]
        pull = factor * factor * ((dots[:8] + dots[8:]) * (1.0 / D))
        both = jnp.concatenate([factor, factor], axis=0), jnp.concatenate([pull, pull], axis=0)
        pack(0, enc_grad[...] + both[0] * (mapped(total, dge) - both[1] * enc_saved[...]), prv)
        for i in range(16):
            x = saved_ref[:, wide(i)].astype(F32)
            scaled = decode_piece(total, i) * gain_ref[:, wide(i)]
            value = grad_ref[:, wide(i)].astype(F32) + factor * (scaled - x * pull)
            ig_ref[:, wide(i)] = value.astype(BF16)
        store(2, ig_ref, ig_hbm)

    def get_grad():
        drain(4)
        received(0, gs_ref, nxt, s < 7)
        store(3, gs_ref, gs_hbm)

    def get_act():
        drain(4)
        received(1, act_ref, prv, s > 0)
        store(1, act_ref, act_hbm)

    tasks = {
        "tables": make_tables,
        "enc": make_enc,
        "maps": make_maps,
        "own": make_encoded,
        "sfin": lambda: project(SAVED, 0),
        "attS": lambda: attend(0),
        "gfin": grad_attended,
        "bwd": attention_back,
        "kvsum": keyval_sum,
        "ffin": lambda: project(FWD, 1),
        "attF": lambda: attend(1),
        "fin0": finish_back,
        "fin1": finish_forward,
        "rcv0": get_grad,
        "rcv1": get_act,
    }
    for i in range(4):
        tasks[f"woe{i}"] = lambda i=i: make_woe(i)
        tasks[f"qe{i}"] = lambda i=i: make_qe(i)
    for a, name in ((SAVED, "s"), (GRAD, "g"), (FWD, "f")):
        for part in range(2):
            tasks[f"{name}x{part}"] = lambda a=a, part=part: swap(a, part)
            for k in range(4):
                tasks[f"{name}{part}{k}"] = lambda a=a, part=part, k=k: contract(a, part, k)
    for name, a, w in (("s", SAVED, 0), ("f", FWD, 1)):
        for part in range(2):
            tasks[f"{name}k{part}"] = lambda a=a, w=w, part=part: keyvals(a, w, part)
    for w, first in enumerate((back_part, fwd_part)):
        for q in range(2):
            tasks[f"sp{w}{q}"] = lambda w=w, q=q, first=first: spread(w, q, first)
            tasks[f"rx{w}{q}"] = lambda w=w, q=q: reduce_x(w, q)
            tasks[f"rz{w}{q}"] = lambda w=w, q=q: reduce_z(w, q)
    formed = set()
    for item in ORDER:
        if isinstance(item, str):
            tasks[item]()
        elif item[0] == "W":
            take(*item[1:])
        else:
            if item[1] not in formed:
                formed.add(item[1])
                form_own(item[1])
            hand(*item[1:])
    drain(0)
    for copy in stores:
        copy.wait()


def hand_over(*refs):
    copies = [pltpu.make_async_copy(refs[i], refs[4 + i], refs[8].at[i]) for i in range(4)]
    for copy in copies:
        copy.start()
    for copy in copies:
        copy.wait()


def on_device(
    fwd_in, saved_in, grad_in, norm_gain, query_weight, keyval_weight, out_weight, encoder, decoder, seq_pos, rope_ids
):
    frequency = np.repeat(ROPE_BASE ** (-2.0 * np.arange(HD // 2) / HD), 2)[None].astype(np.float32)
    operands = [
        fwd_in[0],
        saved_in[0],
        grad_in[0],
        norm_gain,
        jnp.asarray(frequency),
        rope_ids[None],
        seq_pos[None],
        query_weight[0],
        keyval_weight[0].T,
        out_weight[0],
        encoder.transpose(0, 2, 1).reshape(ENC, 128),
        decoder.reshape(ENC, 128),
    ]
    hbm = pl.BlockSpec(memory_space=pl.ANY)
    vmem = pl.BlockSpec(memory_space=pltpu.VMEM)
    dma = pltpu.SemaphoreType.DMA
    shapes = [jax.ShapeDtypeStruct((8, D), BF16)] * 4
    outs = pl.pallas_call(
        kernel,
        out_shape=shapes,
        in_specs=[hbm] * len(operands),
        out_specs=[hbm] * 4,
        scratch_shapes=[pltpu.VMEM((2, *x.shape) if x.shape[0] == 64 else x.shape, x.dtype) for x in operands]
        + [
            pltpu.VMEM((D // 2, 256), BF16),
            pltpu.VMEM((256, HALF), BF16),
        ]
        + [pltpu.VMEM((8, D), BF16)] * 4
        + [
            pltpu.VMEM((3, 2, 8, 16, HALF), BF16),
            pltpu.VMEM((T, HD), F32),
            pltpu.VMEM((T, HD), F32),
            pltpu.VMEM((T, HD), F32),
            pltpu.VMEM((T, HD), F32),
            pltpu.VMEM((T, HD), F32),
            pltpu.VMEM((8, T), F32),
            pltpu.VMEM((D, 128), BF16),
            pltpu.VMEM((ENC, 512), BF16),
            pltpu.VMEM((ENC, 512), BF16),
            pltpu.VMEM((256, ENC), BF16),
            pltpu.VMEM((ENC, 256), BF16),
            pltpu.VMEM((ENC, 128), BF16),
            pltpu.VMEM((ENC, 128), BF16),
            pltpu.VMEM((ENC, 128), BF16),
            pltpu.VMEM((16, ENC // 2), F32),
            pltpu.VMEM((16, ENC // 2), F32),
            pltpu.VMEM((16, ENC // 2), F32),
            pltpu.VMEM((16, ENC // 2), F32),
            pltpu.VMEM((3, 2, 8, HALF), F32),
            pltpu.VMEM((3, 2, 8, HALF), F32),
            pltpu.VMEM((8, 128), F32),
            pltpu.VMEM((3, T, 256), F32),
            pltpu.VMEM((3, T, 128), F32),
            pltpu.VMEM((3, T, 256), F32),
            pltpu.VMEM((3, T, 256), F32),
            pltpu.VMEM((2, 2, 2, 2, HD, 128), BF16),
            pltpu.VMEM((2, 2, HD, T), BF16),
            pltpu.VMEM((2, T, 256), BF16),
            pltpu.VMEM((2, HD, T), BF16),
            pltpu.VMEM((T, 256), BF16),
            pltpu.VMEM((256, T), BF16),
            pltpu.VMEM((2, T, T), F32),
            pltpu.VMEM((T, 256), BF16),
            pltpu.VMEM((T, 256), BF16),
            pltpu.VMEM((T, 128), BF16),
            pltpu.VMEM((2, HD, T), BF16),
            pltpu.VMEM((HD, T), BF16),
            pltpu.VMEM((2, 2, 2, 2, 8, 16, ENC // 4), BF16),
            pltpu.VMEM((2, 2, 2, 8, 16, ENC // 4), BF16),
            pltpu.VMEM((2, 2, 8, 16, ENC // 4), BF16),
            pltpu.VMEM((2, 2, 7, 16, ENC // 4), BF16),
            pltpu.VMEM((2, 2, 2, 8, 2, 16, ENC // 4), BF16),
            pltpu.VMEM((2, 2, 8, 2, 16, ENC // 4), BF16),
            pltpu.VMEM((2, 2, 7, 2, 16, ENC // 4), BF16),
            pltpu.VMEM((2, 2, 16, ENC // 4), BF16),
            pltpu.VMEM((2, 16, ENC // 2), BF16),
            pltpu.VMEM((2, 16, ENC // 2), BF16),
            dma((len(operands),)),
            dma((4,)),
            dma((3,)),
            dma((3,)),
            dma((3,)),
            dma((3,)),
            dma((3, len(KEYS))),
            dma((3, len(KEYS))),
            dma((3, 2)),
            dma((3, 2)),
            dma((2, 2, 3)),
            dma((2, 2, 3)),
            dma(()),
            dma(()),
            dma((2, 2, 9)),
            dma((2, 2, 9)),
            dma((2,)),
            dma((2,)),
        ],
        compiler_params=pltpu.CompilerParams(collective_id=0, has_side_effects=True, vmem_limit_bytes=60 << 20),
        name="relay_tick",
    )(*operands)
    outs = pl.pallas_call(
        hand_over,
        out_shape=shapes,
        in_specs=[vmem] * 4,
        out_specs=[hbm] * 4,
        scratch_shapes=[dma((4,))],
        name="hand_over",
    )(*outs)
    return tuple(o[None] for o in outs)


def solution(mesh):
    rows = P("section", "tensor", None)
    columns = P("section", None, "tensor")
    return jax.shard_map(
        on_device,
        mesh=mesh,
        in_specs=(rows, rows, rows, P("section", None), columns, columns, rows, P(), P(), P(), P()),
        out_specs=(rows, rows, rows, rows),
        check_vma=False,
    )
```

```python
import math

import jax
import jax.numpy as jnp
import numpy as np
from jax import lax
from jax.experimental import pallas as pl
from jax.experimental.pallas import tpu as pltpu
from jax.sharding import PartitionSpec as P

MESH = pl.DeviceIdType.MESH
HD = 128
D = 8192
HALF = D // 2
ENC = 2048
T = 256
EPSILON = 1e-05
ROPE_BASE = 10000.0
NEG_FILL = -1e30
SCALE = 1.0 / math.sqrt(HD)
F32 = jnp.float32
BF16 = jnp.bfloat16
SAVED, GRAD, FWD = 0, 1, 2
Z_FIRST = ((1, 1),)

KEYS = [(0, 1), (0, -1), (0, 2), (0, -2), (0, 3), (0, -3), (0, 4, 0), (0, 4, 1)]
KEYS += [(1, 0), (1, 1), (1, -1), (1, 2), (1, -2), (1, 3), (1, -3), (1, 4, 0), (1, 4, 1)]
COLUMNS = [[k for k in KEYS if k[0] == 0], [k for k in KEYS if k[0] == 1]]
ORDER = [
    ("S", 0, "M", (0, 0)), ("S", 0, "P", (0, 0)), ("S", 0, "X", (0, 0)), "tables", ("S", 1, "M", (0, 0)),
    ("S", 1, "P", (0, 0)), ("S", 1, "X", (0, 0)), "enc", ("S", 2, "M", (0, 0)), ("S", 2, "P", (0, 0)),
    ("S", 2, "X", (0, 0)), "woe0", ("W", 0, (0, 1)), ("S", 0, "M", (0, 1)), ("W", 0, (0, -1)),
    ("S", 0, "P", (0, -1)), ("S", 0, "X", (0, 1)), "woe1", "woe2", ("S", 0, "X", (0, -1)), "woe3",
    ("W", 1, (0, 1)), ("S", 1, "M", (0, 1)), ("W", 1, (0, -1)), ("S", 1, "P", (0, -1)), "qe0", "qe1",
    ("S", 1, "X", (0, 1)), ("W", 2, (0, 1)), ("S", 2, "M", (0, 1)), ("W", 2, (0, -1)), ("S", 2, "P", (0, -1)),
    "qe2", "qe3", "maps", ("W", 0, (0, 2)), ("S", 0, "M", (0, 2)), ("W", 0, (0, -2)), ("S", 0, "P", (0, -2)),
    ("S", 0, "X", (0, 2)), "own", ("S", 0, "X", (0, -2)), ("W", 1, (0, 2)), ("S", 1, "M", (0, 2)),
    ("W", 1, (0, -2)), ("S", 1, "P", (0, -2)), ("S", 1, "X", (0, 2)), ("W", 2, (0, 2)), ("S", 2, "M", (0, 2)),
    ("W", 2, (0, -2)), ("S", 2, "P", (0, -2)), ("S", 1, "X", (0, -2)), ("W", 0, (0, 3)), ("S", 0, "M", (0, 3)),
    ("W", 0, (0, -3)), ("S", 0, "P", (0, -3)), ("W", 0, (1, 2)), ("S", 0, "M", (1, 2)), ("S", 2, "X", (0, 2)),
    ("W", 1, (0, -3)), ("S", 1, "P", (0, -3)), ("W", 0, (1, -2)), ("S", 0, "P", (1, -2)), ("W", 1, (0, 3)),
    ("S", 1, "M", (0, 3)), ("S", 2, "X", (0, -2)), ("W", 2, (0, 3)), ("S", 2, "M", (0, 3)), ("W", 2, (0, -3)),
    ("S", 2, "P", (0, -3)), ("W", 1, (1, 2)), ("S", 1, "M", (1, 2)), ("W", 0, (0, 4, 0)), ("W", 0, (0, 4, 1)),
    "s00", "s01", ("S", 1, "X", (0, -1)), "s02", ("W", 1, (1, -2)), ("S", 1, "P", (1, -2)), "s03", "sk0", "sx0",
    ("W", 0, (1, 3)), ("S", 0, "M", (1, 3)), ("W", 1, (0, 4, 0)), ("W", 1, (0, 4, 1)), "g00", ("W", 0, (1, -3)),
    ("S", 0, "P", (1, -3)), ("W", 2, (1, 2)), ("S", 2, "M", (1, 2)), "g01", ("S", 2, "X", (0, 1)), "g02", "g03",
    "gx0", ("W", 2, (0, 4, 0)), ("W", 2, (0, 4, 1)), "f00", "f01", ("W", 2, (1, -2)), ("S", 2, "P", (1, -2)),
    "f02", ("S", 2, "X", (0, -1)), "f03", ("W", 1, (1, 3)), ("S", 1, "M", (1, 3)), ("W", 1, (1, -3)),
    ("S", 1, "P", (1, -3)), "fk0", "fx0", ("W", 0, (1, 0)), ("W", 0, (1, 1)), ("W", 0, (1, -1)),
    ("W", 0, (1, 4, 0)), ("W", 0, (1, 4, 1)), "s10", "s11", "s12", "s13", "sk1", "sx1", ("W", 2, (1, 3)),
    ("S", 2, "M", (1, 3)), ("W", 2, (1, -3)), ("S", 2, "P", (1, -3)), ("W", 1, (1, 0)), ("W", 1, (1, 1)),
    ("W", 1, (1, -1)), ("W", 1, (1, 4, 0)), ("W", 1, (1, 4, 1)), "g10", "g11", "g12", "g13", "gx1", "sfin",
    ("W", 2, (1, 0)), ("W", 2, (1, 1)), ("W", 2, (1, -1)), ("W", 2, (1, 4, 0)), ("W", 2, (1, 4, 1)), "f10", "f11",
    "f12", "f13", "fk1", "fx1", "gfin", "attS", "bwd", "ffin", "attF", "sp11", "sp10", "kvsum", "sp01", "sp00",
    "rz11", "rx10", "rx01", "rx00", "rz10", "rx11", "rz01", "rz00",
    "fin1", "fin0", "outs", "rcv1", "rcv0",
]


def mm(a, b):
    return jnp.dot(a, b, preferred_element_type=F32)


def mm_nt(a, b):
    return lax.dot_general(a, b, (((1,), (1,)), ((), ())), preferred_element_type=F32)


def rotate(x, cosine, sine):
    lane = lax.broadcasted_iota(jnp.int32, x.shape, 1)
    swapped = jnp.where(lane % 2 == 0, pltpu.roll(x, x.shape[1] - 1, 1), pltpu.roll(x, 1, 1))
    return x * cosine + swapped * sine


def kernel(
    fwd_hbm, saved_hbm, grad_hbm, gain_hbm, freq_hbm, rope_hbm, seq_hbm, wq_hbm, wkv_hbm, wo_hbm, enc_hbm, dec_hbm,
    out_hbm, act_hbm, ig_hbm, gs_hbm,
    fwd_ref, saved_ref, grad_ref, gain_ref, freq_ref, rope_ref, seq_ref, wq, wkv, wo, enc_raw, dec_raw, wqs, wos,
    out_ref, act_ref, ig_ref, gs_ref,
    G, cos_ref, sin_ref, kvcos_ref, kvsin_ref, seqc_ref, seqr_ref, enc_bd, enc_t, dec_bd, woe, qe, kve, de, dge, enc_fwd, enc_saved, enc_grad, pull_ref,
    nrm, chipf, factor_ref, acc, acckv, other, got, kvp, kvt, qrot, qtr, gab, gatr, prob, att, qg, kvg, kgs, kgr,
    rsb, r1, r2, r3, rz, rz1, rz3, rz2, pk_s, pk_r,
    wsem, osem, ws_s, ws_r, st_s, st_r, g_s, g_r, sb_s, sb_r, kv_s, kv_r, kg_s, kg_r, rs_s, rs_r, sc_s, sc_r,
):
    s = lax.axis_index("section")
    t = lax.axis_index("tensor")
    z, h, c = t // 4, (t // 2) % 2, t % 2

    def tid(zz, hh, cc):
        return (s, zz * 4 + hh * 2 + cc)

    def zmod(d):
        return lax.rem(z + d + 8, 8)

    sib = tid(z, h, 1 - c)
    link = {"M": tid(zmod(-1), h, c), "P": tid(zmod(1), h, c), "X": tid(z, 1 - h, c)}
    group = [sib, link["X"], tid(z, 1 - h, 1 - c)]
    nxt, prv = (lax.rem(s + 1, 8), t), (lax.rem(s + 7, 8), t)
    along = [tid(zmod(k), h, c) for k in range(1, 8)]

    arrays = {
        "saved": (saved_hbm, saved_ref), "gain": (gain_hbm, gain_ref), "grad": (grad_hbm, grad_ref), "fwd": (fwd_hbm, fwd_ref),
        "rope": (rope_hbm, rope_ref), "seq": (seq_hbm, seq_ref), "freq": (freq_hbm, freq_ref),
        "enc": (enc_hbm, enc_raw), "dec": (dec_hbm, dec_raw), "wo": (wo_hbm, wo), "wq": (wq_hbm, wq), "wkv": (wkv_hbm, wkv.at[c]),
    }
    loads = {}
    for i, (name, (src, dst)) in enumerate(arrays.items()):
        loads[name] = pltpu.make_async_copy(src, dst, wsem.at[i])
        if i < 4:
            loads[name].start()

    barrier = pltpu.get_barrier_semaphore()
    for peer in along + group + [nxt, prv]:
        pl.semaphore_signal(barrier, inc=1, device_id=peer, device_id_type=MESH)

    def put_own(a, values):
        nrm[a, 0] = values[:, :HALF]
        nrm[a, 1] = values[:, HALF:]

    def normed(ref, slot):
        x = ref[...].astype(F32)
        factor = lax.rsqrt(jnp.mean(x * x, axis=-1, keepdims=True) + EPSILON)
        if slot is not None:
            factor_ref[...] = jnp.broadcast_to(factor, factor_ref.shape)
        return x * factor * gain_ref[...]

    pending, stores = [], []

    def store(i, src, dst):
        stores.append(pltpu.make_async_copy(src, dst, osem.at[i]))
        stores[-1].start()

    def send(src, dst, ssem, rsem, peer):
        copy = pltpu.make_async_remote_copy(
            src_ref=src, dst_ref=dst, send_sem=ssem, recv_sem=rsem, device_id=peer, device_id_type=MESH
        )
        copy.start()
        pending.append(copy)

    def drain(keep):
        while len(pending) > keep:
            pending.pop(0).wait_send()

    def arrived(dst, ssem, rsem, peer):
        pltpu.make_async_remote_copy(
            src_ref=dst, dst_ref=dst, send_sem=ssem, recv_sem=rsem, device_id=peer, device_id_type=MESH
        ).wait_recv()

    def stage(a):
        send(nrm.at[a, 1 - c], chipf.at[a, c], st_s.at[a], st_r.at[a], sib)

    loads["saved"].wait()
    loads["gain"].wait()
    put_own(SAVED, normed(saved_ref, 0))
    pl.semaphore_wait(barrier, len(along) + len(group) + 2)
    stage(SAVED)
    for name in list(arrays)[4:]:
        loads[name].start()
    loads["grad"].wait()
    put_own(GRAD, grad_ref[...].astype(F32))
    stage(GRAD)
    loads["fwd"].wait()
    put_own(FWD, normed(fwd_ref, None))
    stage(FWD)

    away = pl.ds(pl.multiple_of((1 - c) * HALF, HALF), HALF)
    shared = [(wq_hbm.at[away, :], wqs), (wkv_hbm, wkv.at[c]), (wo_hbm.at[:, away], wos)]
    for i, (src, dst) in enumerate(shared):
        send(src, dst, ws_s.at[i], ws_r.at[i], sib)

    ready = set()

    def need(*names):
        for name in names:
            if name in ready:
                continue
            ready.add(name)
            if isinstance(name, int):
                dst = wkv.at[1 - c] if name == 1 else shared[name][1]
                arrived(dst, ws_s.at[name], ws_r.at[name], sib)
            else:
                loads[name].wait()

    def make_tables():
        need("rope", "seq", "freq")

        def down(row):
            tall = jnp.broadcast_to(row.astype(F32), (128, T)).T
            return jnp.concatenate([tall[zz * 32 + hh * 16 :][:16] for hh in range(2) for zz in range(8)], axis=0)

        positions = down(seq_ref[...])
        seqc_ref[...] = positions
        seqr_ref[...] = positions.T[:8]
        angle = down(rope_ref[...]) * freq_ref[...]
        cosine, sine = jnp.cos(angle), jnp.sin(angle)
        sine = jnp.where(lax.broadcasted_iota(jnp.int32, sine.shape, 1) % 2 == 0, -sine, sine)
        cos_ref[...] = cosine
        sin_ref[...] = sine
        is_key = jnp.where(h == 0, 1.0, 0.0)
        kvcos_ref[...] = is_key * cosine + (1.0 - is_key)
        kvsin_ref[...] = is_key * sine

    def where(key):
        return (h if key[0] == 0 else 1 - h), zmod(key[1])

    def piece(a, key):
        ref = G.at[(a, *where(key))]
        if len(key) == 3:
            ref = ref.at[:, pl.ds(key[2] * (HALF // 2), HALF // 2)]
        return ref

    def form_own(a):
        arrived(chipf.at[a, 1 - c], st_s.at[a], st_r.at[a], sib)
        chipf[a, c] = nrm[a, c]
        G[a, h, z] = chipf[a].reshape(16, HALF).astype(BF16)

    def take(a, key):
        i = KEYS.index(key)
        arrived(piece(a, key), g_s.at[a, i], g_r.at[a, i], link["M"])

    def hand(a, way, key):
        column, far = (key[0], key[1] + (1 if way == "M" else -1)) if way != "X" else (1 - key[0], key[1])
        there = (column, 4, 0 if way == "M" else 1) if abs(far) == 4 else (column, far)
        i = KEYS.index(there)
        part = piece(a, key + there[2:])
        send(part, part, g_s.at[a, i], g_r.at[a, i], link[way])

    def make_enc():
        need("enc", "dec")

        def fill(i, _):
            rows = pl.ds(i * 128, 128)
            group_row = lax.broadcasted_iota(jnp.int32, (128, 128), 0) // 32
            e, d = enc_raw[rows, :], dec_raw[rows, :]
            wide = jnp.concatenate([jnp.where(group_row == q, e, 0.0) for q in range(4)], axis=1)
            enc_t[rows, :] = wide.astype(BF16)
            enc_bd[pl.ds(i * 512, 512), :] = wide.T.astype(BF16)
            wide = jnp.concatenate([jnp.where(group_row == q, d, 0.0) for q in range(4)], axis=1)
            dec_bd[rows, :] = wide.astype(BF16)
            return 0

        lax.fori_loop(0, 16, fill, 0)

    def make_woe(part):
        need("wo")

        def fill(i, _):
            cols = pl.ds(pl.multiple_of(i * 512, 512), 512)
            outs = pl.ds(pl.multiple_of(i * 128, 128), 128)
            woe[:, outs] = mm(wo[:, cols], enc_bd[pl.ds(i * 512, 512), :]).astype(BF16)
            return 0

        lax.fori_loop(part * 4, part * 4 + 4, fill, 0)

    def make_qe(part):
        need("wq", "wkv", 1)

        def fill(i, _):
            rows, outs = pl.ds(i * 512, 512), pl.ds(i * 128, 128)
            e = enc_t[outs, :]
            qe[outs, :] = mm(e, wq[rows, :]).astype(BF16)
            kve[outs, :] = mm_nt(e, wkv[:, :, pl.ds(pl.multiple_of(i * 512, 512), 512)].reshape(128, 512)).astype(BF16)
            return 0

        lax.fori_loop(part * 4, part * 4 + 4, fill, 0)

    def rows_of(part):
        return pl.ds(pl.multiple_of((h if part == 0 else 1 - h) * 128, 128), 128)

    def contract(a, part, k):
        need(*(("wo", 2) if a == GRAD else ("wq", "wkv", 0, 1)))
        rows, cols = rows_of(part), slice(k * 1024, k * 1024 + 1024)
        here = pl.ds(pl.multiple_of(c * HALF + k * 1024, 1024), 1024)
        x = G[a, h if part == 0 else 1 - h, :, :, cols].reshape(128, 1024)
        if a == GRAD:
            products = [(acc, mm_nt(x, wo[:, here])), (other, mm_nt(x, wos[:, cols]))]
        else:
            products = [(acc, mm(x, wq[here, :])), (other, mm(x, wqs[cols, :])), (acckv, mm_nt(x, wkv[:, :, here].reshape(128, 1024)))]
        for ref, product in products:
            if k == 0:
                ref[a, rows, :] = product
            else:
                ref[a, rows, :] += product

    def swap(a, part):
        rows = rows_of(part)
        send(other.at[a, rows], got.at[a, rows], sb_s.at[a, part], sb_r.at[a, part], sib)

    def swapped(a):
        for part in range(2):
            rows = rows_of(part)
            arrived(got.at[a, rows], sb_s.at[a, part], sb_r.at[a, part], sib)

    def keyvals(a, w, part):
        rows, col = rows_of(part), h if part == 0 else 1 - h
        turned = rotate(acckv[a, rows, :], kvcos_ref[rows, :], kvsin_ref[rows, :])
        mine = kvp.at[w, h, c, col]
        mine[...] = turned.T.astype(BF16)
        for i, peer in enumerate(group):
            send(mine, mine, kv_s.at[w, part, i], kv_r.at[w, part, i], peer)

    def keyvals_in(w):
        for part in range(2):
            col = h if part == 0 else 1 - h
            for i, (hh, cc) in enumerate([(h, 1 - c), (1 - h, c), (1 - h, 1 - c)]):
                arrived(kvp.at[w, hh, cc, col], kv_s.at[w, part, i], kv_r.at[w, part, i], group[i])
        for hh in range(2):
            for col in range(2):
                total = kvp[w, hh, 0, col].astype(F32) + kvp[w, hh, 1, col].astype(F32)
                kvt[w, hh, :, col * 128 : col * 128 + 128] = total.astype(BF16)

    def project(a, w):
        swapped(a)
        for i in range(2):
            cols = slice(i * HD, (i + 1) * HD)
            q = rotate(acc[a, :, cols] + got[a, :, cols], cos_ref[...], sin_ref[...])
            qrot[w, :, cols] = q.astype(BF16)
            if w == 0:
                qtr[i] = q.T.astype(BF16)

    def attend(w):
        keyvals_in(w)
        kt, vt = kvt[w, 0], kvt[w, 1]
        visible = seqr_ref[:1, :] <= seqc_ref[:, :1]
        for i in range(2):
            cols = slice(i * HD, (i + 1) * HD)
            scores = jnp.where(visible, mm(qrot[w, :, cols], kt) * SCALE, NEG_FILL)
            raised = jnp.exp(scores - jnp.max(scores, axis=-1, keepdims=True))
            p = raised / jnp.sum(raised, axis=-1, keepdims=True)
            if w == 0:
                prob[i] = p
            else:
                att[:, cols] = mm_nt(p.astype(BF16), vt).astype(BF16)

    def grad_attended():
        swapped(GRAD)
        total = acc[GRAD] + got[GRAD]
        gab[...] = total.astype(BF16)
        gatr[...] = total.T.astype(BF16)

    def attention_back():
        kt, vt = kvt[0, 0], kvt[0, 1]
        key_sum = jnp.zeros((HD, T), F32)
        value_sum = jnp.zeros((HD, T), F32)
        for i in range(2):
            cols = slice(i * HD, (i + 1) * HD)
            p = prob[i]
            dp = mm(gab[:, cols], vt)
            sg = (p * (dp - jnp.sum(p * dp, axis=-1, keepdims=True)) * SCALE).astype(BF16)
            qg[:, cols] = rotate(mm_nt(sg, kt), cos_ref[...], -sin_ref[...]).astype(BF16)
            key_sum += mm(qtr[i], sg)
            value_sum += mm(gatr[cols, :], p.astype(BF16))
        kgs[0] = key_sum.astype(BF16)
        kgs[1] = value_sum.astype(BF16)
        send(kgs.at[1 - h], kgr, kg_s, kg_r, link["X"])

    def keyval_sum():
        arrived(kgr, kg_s, kg_r, link["X"])
        total = kgs[h].astype(F32) + kgr[...].astype(F32)
        kvg[...] = rotate(total.T, kvcos_ref[...], -kvsin_ref[...]).astype(BF16)

    def spread(w, q, first):
        def chunk(k, _):
            at = pl.multiple_of(q * 512 + k * 256, 256)
            lows, highs = first(at), first(at + ENC // 2)
            cols = pl.ds(pl.multiple_of(k * 256, 256), 256)
            for b in range(32):
                hh, zz, cc = b // 16, (b // 2) % 8, b % 2
                rows = slice(b * 8, b * 8 + 8)
                both = jnp.concatenate([lows[rows], highs[rows]], axis=0).astype(BF16)
                if (w, q) in Z_FIRST:
                    rz[w, q, cc, zz, hh, :, cols] = both
                else:
                    rsb[w, q, cc, hh, zz, :, cols] = both
            return 0

        lax.fori_loop(0, 2, chunk, 0)
        src, dst = (rz, rz1) if (w, q) in Z_FIRST else (rsb, r1)
        send(src.at[w, q, 1 - c], dst.at[w, q], rs_s.at[w, q, 0], rs_r.at[w, q, 0], sib)

    def fwd_part(at):
        return mm(att[...], woe[:, pl.ds(at, 256)])

    def back_part(at):
        return mm_nt(qg[...], qe[pl.ds(at, 256), :]) + mm_nt(kvg[...], kve[pl.ds(at, 256), :])

    def from_core(w, q):
        arrived((rz1 if (w, q) in Z_FIRST else r1).at[w, q], rs_s.at[w, q, 0], rs_r.at[w, q, 0], sib)

    def along_z(w, q, slots, total):
        for k in range(1, 8):
            arrived(slots.at[w, q, k - 1], rs_s.at[w, q, 1 + k], rs_r.at[w, q, 1 + k], along[k - 1])
            total += slots[w, q, k - 1].astype(F32)
        return total

    def reduce_x(w, q):
        sems = rs_s.at[w, q, 1], rs_r.at[w, q, 1]
        if (w, q) in Z_FIRST:
            rz[w, q, c, z] = along_z(w, q, rz3, rz[w, q, c, z].astype(F32)).astype(BF16)
            send(rz.at[w, q, c, z, 1 - h], rz2.at[w, q], *sems, link["X"])
        else:
            from_core(w, q)
            rsb[w, q, c, 1 - h] = (rsb[w, q, c, 1 - h].astype(F32) + r1[w, q, 1 - h].astype(F32)).astype(BF16)
            send(rsb.at[w, q, c, 1 - h], r2.at[w, q], *sems, link["X"])

    def reduce_z(w, q):
        if (w, q) in Z_FIRST:
            from_core(w, q)
            rz[w, q, c] = (rz[w, q, c].astype(F32) + rz1[w, q].astype(F32)).astype(BF16)
        else:
            arrived(r2.at[w, q], rs_s.at[w, q, 1], rs_r.at[w, q, 1], link["X"])
            total = rsb[w, q, c, h].astype(F32) + r1[w, q, h].astype(F32) + r2[w, q].astype(F32)
            rsb[w, q, c, h] = total.astype(BF16)
        for k in (4, 3, 5, 2, 6, 1, 7):
            sems = rs_s.at[w, q, 1 + k], rs_r.at[w, q, 1 + k]
            if (w, q) in Z_FIRST:
                send(rz.at[w, q, c, zmod(k)], rz3.at[w, q, k - 1], *sems, along[k - 1])
            else:
                send(rsb.at[w, q, c, h, zmod(k)], r3.at[w, q, k - 1], *sems, along[k - 1])

    def reduced(w):
        totals = []
        for q in range(2):
            if (w, q) in Z_FIRST:
                arrived(rz2.at[w, q], rs_s.at[w, q, 1], rs_r.at[w, q, 1], link["X"])
                totals.append(rz[w, q, c, z, h].astype(F32) + rz2[w, q].astype(F32))
            else:
                totals.append(along_z(w, q, r3, rsb[w, q, c, h, z].astype(F32)))
        return jnp.concatenate(totals, axis=1)

    def part_of(i):
        return slice((i // 8) * 8, (i // 8) * 8 + 8), slice((i % 8) * 128, (i % 8) * 128 + 128)

    def wide(i):
        return slice(i * 512, i * 512 + 512)

    def each_group(make):
        return [jnp.concatenate([make(i), make(i + 8)], axis=0) for i in range(8)]

    def decode_piece(encoded, i):
        return mm(encoded[part_of(i)].astype(BF16), dec_bd[i * 128 : i * 128 + 128, :])

    def make_maps():
        def fill(i, _):
            rows, cols = pl.ds(i * 128, 128), pl.ds(pl.multiple_of(i * 512, 512), 512)
            d, e = dec_bd[rows, :], enc_bd[pl.ds(i * 512, 512), :]
            de[rows, :] = mm(d, e).astype(BF16)
            dge[rows, :] = mm((d.astype(F32) * gain_ref[:, cols]).astype(BF16), e).astype(BF16)
            return 0

        lax.fori_loop(0, 16, fill, 0)

    def make_encoded():
        def encode(ref):
            return each_group(lambda i: mm(ref[:, wide(i)], enc_bd[i * 512 : i * 512 + 512, :]))

        def pull(i):
            x = saved_ref[:, wide(i)].astype(F32) * gain_ref[:, wide(i)]
            return mm_nt(x.astype(BF16), dec_bd[i * 128 : i * 128 + 128, :])

        for i, parts in enumerate(zip(encode(fwd_ref), encode(saved_ref), encode(grad_ref), each_group(pull))):
            for ref, value in zip((enc_fwd, enc_saved, enc_grad, pull_ref), parts):
                ref[:, i * 128 : i * 128 + 128] = value

    def pack(w, values, peer):
        pk_s[w] = values.astype(BF16)
        send(pk_s.at[w], pk_r.at[w], sc_s.at[w], sc_r.at[w], peer)

    def mapped(total, table):
        parts = each_group(lambda i: mm(total[part_of(i)].astype(BF16), table[i * 128 : i * 128 + 128, :]))
        return jnp.concatenate(parts, axis=1)

    def received(w, out, peer, keep):
        arrived(pk_r.at[w], sc_s.at[w], sc_r.at[w], peer)
        got = pk_r[w].astype(F32)
        got = got * jnp.where(keep, 1.0, 0.0)
        for i in range(16):
            out[:, wide(i)] = decode_piece(got, i).astype(BF16)

    left = []

    def put_outs():
        while left:
            left.pop(0)()

    def finish_forward():
        drain(40)
        total = reduced(1)
        pack(1, enc_fwd[...] + mapped(total, de), nxt)

        def put_out():
            for i in range(16):
                out_ref[:, wide(i)] = (fwd_ref[:, wide(i)].astype(F32) + decode_piece(total, i)).astype(BF16)
            store(0, out_ref, out_hbm)

        left.append(put_out)

    def finish_back():
        drain(40)
        total = reduced(0)
        dots = jnp.sum(total * pull_ref[...], axis=-1, keepdims=True)
        factor = factor_ref[:, :1]
        pull = factor * factor * ((dots[:8] + dots[8:]) * (1.0 / D))
        both = jnp.concatenate([factor, factor], axis=0), jnp.concatenate([pull, pull], axis=0)
        pack(0, enc_grad[...] + both[0] * (mapped(total, dge) - both[1] * enc_saved[...]), prv)

        def put_out():
            for i in range(16):
                x = saved_ref[:, wide(i)].astype(F32)
                scaled = decode_piece(total, i) * gain_ref[:, wide(i)]
                value = grad_ref[:, wide(i)].astype(F32) + factor * (scaled - x * pull)
                ig_ref[:, wide(i)] = value.astype(BF16)
            store(2, ig_ref, ig_hbm)

        left.append(put_out)

    def get_grad():
        drain(4)
        received(0, gs_ref, nxt, s < 7)
        store(3, gs_ref, gs_hbm)

    def get_act():
        drain(4)
        received(1, act_ref, prv, s > 0)
        store(1, act_ref, act_hbm)

    tasks = {
        "tables": make_tables,
        "enc": make_enc,
        "maps": make_maps,
        "own": make_encoded,
        "sfin": lambda: project(SAVED, 0),
        "attS": lambda: attend(0),
        "gfin": grad_attended,
        "bwd": attention_back,
        "kvsum": keyval_sum,
        "ffin": lambda: project(FWD, 1),
        "attF": lambda: attend(1),
        "fin0": finish_back,
        "fin1": finish_forward,
        "outs": put_outs,
        "rcv0": get_grad,
        "rcv1": get_act,
    }
    for i in range(4):
        tasks[f"woe{i}"] = lambda i=i: make_woe(i)
        tasks[f"qe{i}"] = lambda i=i: make_qe(i)
    for a, name in ((SAVED, "s"), (GRAD, "g"), (FWD, "f")):
        for part in range(2):
            tasks[f"{name}x{part}"] = lambda a=a, part=part: swap(a, part)
            for k in range(4):
                tasks[f"{name}{part}{k}"] = lambda a=a, part=part, k=k: contract(a, part, k)
    for name, a, w in (("s", SAVED, 0), ("f", FWD, 1)):
        for part in range(2):
            tasks[f"{name}k{part}"] = lambda a=a, w=w, part=part: keyvals(a, w, part)
    for w, first in enumerate((back_part, fwd_part)):
        for q in range(2):
            tasks[f"sp{w}{q}"] = lambda w=w, q=q, first=first: spread(w, q, first)
            tasks[f"rx{w}{q}"] = lambda w=w, q=q: reduce_x(w, q)
            tasks[f"rz{w}{q}"] = lambda w=w, q=q: reduce_z(w, q)
    formed = set()
    for item in ORDER:
        if isinstance(item, str):
            tasks[item]()
        elif item[0] == "W":
            take(*item[1:])
        else:
            if item[1] not in formed:
                formed.add(item[1])
                form_own(item[1])
            hand(*item[1:])
    drain(0)
    for copy in stores:
        copy.wait()


def hand_over(*refs):
    copies = [pltpu.make_async_copy(refs[i], refs[4 + i], refs[8].at[i]) for i in range(4)]
    for copy in copies:
        copy.start()
    for copy in copies:
        copy.wait()


def on_device(
    fwd_in, saved_in, grad_in, norm_gain, query_weight, keyval_weight, out_weight, encoder, decoder, seq_pos, rope_ids
):
    frequency = np.repeat(ROPE_BASE ** (-2.0 * np.arange(HD // 2) / HD), 2)[None].astype(np.float32)
    operands = [
        fwd_in[0],
        saved_in[0],
        grad_in[0],
        norm_gain,
        jnp.asarray(frequency),
        rope_ids[None],
        seq_pos[None],
        query_weight[0],
        keyval_weight[0].T,
        out_weight[0],
        encoder.transpose(0, 2, 1).reshape(ENC, 128),
        decoder.reshape(ENC, 128),
    ]
    hbm = pl.BlockSpec(memory_space=pl.ANY)
    vmem = pl.BlockSpec(memory_space=pltpu.VMEM)
    dma = pltpu.SemaphoreType.DMA
    shapes = [jax.ShapeDtypeStruct((8, D), BF16)] * 4
    outs = pl.pallas_call(
        kernel,
        out_shape=shapes,
        in_specs=[hbm] * len(operands),
        out_specs=[hbm] * 4,
        scratch_shapes=[pltpu.VMEM((2, *x.shape) if x.shape[0] == 64 else x.shape, x.dtype) for x in operands]
        + [
            pltpu.VMEM((D // 2, 256), BF16),
            pltpu.VMEM((256, HALF), BF16),
        ]
        + [pltpu.VMEM((8, D), BF16)] * 4
        + [
            pltpu.VMEM((3, 2, 8, 16, HALF), BF16),
            pltpu.VMEM((T, HD), F32),
            pltpu.VMEM((T, HD), F32),
            pltpu.VMEM((T, HD), F32),
            pltpu.VMEM((T, HD), F32),
            pltpu.VMEM((T, HD), F32),
            pltpu.VMEM((8, T), F32),
            pltpu.VMEM((D, 128), BF16),
            pltpu.VMEM((ENC, 512), BF16),
            pltpu.VMEM((ENC, 512), BF16),
            pltpu.VMEM((256, ENC), BF16),
            pltpu.VMEM((ENC, 256), BF16),
            pltpu.VMEM((ENC, 128), BF16),
            pltpu.VMEM((ENC, 128), BF16),
            pltpu.VMEM((ENC, 128), BF16),
            pltpu.VMEM((16, ENC // 2), F32),
            pltpu.VMEM((16, ENC // 2), F32),
            pltpu.VMEM((16, ENC // 2), F32),
            pltpu.VMEM((16, ENC // 2), F32),
            pltpu.VMEM((3, 2, 8, HALF), F32),
            pltpu.VMEM((3, 2, 8, HALF), F32),
            pltpu.VMEM((8, 128), F32),
            pltpu.VMEM((3, T, 256), F32),
            pltpu.VMEM((3, T, 128), F32),
            pltpu.VMEM((3, T, 256), F32),
            pltpu.VMEM((3, T, 256), F32),
            pltpu.VMEM((2, 2, 2, 2, HD, 128), BF16),
            pltpu.VMEM((2, 2, HD, T), BF16),
            pltpu.VMEM((2, T, 256), BF16),
            pltpu.VMEM((2, HD, T), BF16),
            pltpu.VMEM((T, 256), BF16),
            pltpu.VMEM((256, T), BF16),
            pltpu.VMEM((2, T, T), F32),
            pltpu.VMEM((T, 256), BF16),
            pltpu.VMEM((T, 256), BF16),
            pltpu.VMEM((T, 128), BF16),
            pltpu.VMEM((2, HD, T), BF16),
            pltpu.VMEM((HD, T), BF16),
            pltpu.VMEM((2, 2, 2, 2, 8, 16, ENC // 4), BF16),
            pltpu.VMEM((2, 2, 2, 8, 16, ENC // 4), BF16),
            pltpu.VMEM((2, 2, 8, 16, ENC // 4), BF16),
            pltpu.VMEM((2, 2, 7, 16, ENC // 4), BF16),
            pltpu.VMEM((2, 2, 2, 8, 2, 16, ENC // 4), BF16),
            pltpu.VMEM((2, 2, 8, 2, 16, ENC // 4), BF16),
            pltpu.VMEM((2, 2, 7, 2, 16, ENC // 4), BF16),
            pltpu.VMEM((2, 2, 16, ENC // 4), BF16),
            pltpu.VMEM((2, 16, ENC // 2), BF16),
            pltpu.VMEM((2, 16, ENC // 2), BF16),
            dma((len(operands),)),
            dma((4,)),
            dma((3,)),
            dma((3,)),
            dma((3,)),
            dma((3,)),
            dma((3, len(KEYS))),
            dma((3, len(KEYS))),
            dma((3, 2)),
            dma((3, 2)),
            dma((2, 2, 3)),
            dma((2, 2, 3)),
            dma(()),
            dma(()),
            dma((2, 2, 9)),
            dma((2, 2, 9)),
            dma((2,)),
            dma((2,)),
        ],
        compiler_params=pltpu.CompilerParams(collective_id=0, has_side_effects=True, vmem_limit_bytes=60 << 20),
        name="relay_tick",
    )(*operands)
    outs = pl.pallas_call(
        hand_over,
        out_shape=shapes,
        in_specs=[vmem] * 4,
        out_specs=[hbm] * 4,
        scratch_shapes=[dma((4,))],
        name="hand_over",
    )(*outs)
    return tuple(o[None] for o in outs)


def solution(mesh):
    rows = P("section", "tensor", None)
    columns = P("section", None, "tensor")
    return jax.shard_map(
        on_device,
        mesh=mesh,
        in_specs=(rows, rows, rows, P("section", None), columns, columns, rows, P(), P(), P(), P()),
        out_specs=(rows, rows, rows, rows),
        check_vma=False,
    )
```
